128 devices in a mesh: in: 4 (over z_hi, core), out: 4 (over x), tok: 8 (over y, z_lo).
Axes of the slice: x: 4, y: 4, z: 4 (z_hi: 2, z_lo: 2; z = z_hi * 2 + z_lo), core: 2. Of those that a mesh axis runs over, the one named last changes fastest.
Arguments:
- inputs: bfloat16 [2048, 12288], P('tok', 'in'), may hold values from -6 to 6
- out_grad: bfloat16 [2048, 12288], P('tok', 'in'), may hold values from -2 to 2
- w_gate: bfloat16 [12288, 4096], P('in', ('out', 'tok')), may hold values from -0.0546875 to 0.0546875
- w_up: bfloat16 [12288, 4096], P('in', ('out', 'tok')), may hold values from -0.0546875 to 0.0546875
- w_down: bfloat16 [4096, 12288], P('out', ('in', 'tok')), may hold values from -0.09375 to 0.09375
Outputs:
- d_inputs: bfloat16 [2048, 12288], P('tok', ('in', 'out'))
- grad_gate: bfloat16 [12288, 4096], P('in', ('out', 'tok'))
- grad_up: bfloat16 [12288, 4096], P('in', ('out', 'tok'))
- grad_down: bfloat16 [4096, 12288], P('out', ('in', 'tok'))
The draws below stay inside these ranges and needn't reach their ends.
All inputs are finite; a program needn't handle non-finite values.
Results may differ from the reference program's by a relative error of at most 0.0049.
Values may be sent and summed in bfloat16 or wider, within the bound.
A program may use at most 128 MiB of HBM per device.

```python
import jax
import jax.numpy as jnp

D = 12288
FF = 4096
TOKENS = 2048


def level_of(rng, shape, shards, smallest, top_value):
    level = 1.0
    for axis_at, blocks in shards:
        heights = jax.random.uniform(jax.random.fold_in(jax.random.fold_in(rng, 6), axis_at), (blocks,), jnp.float32, smallest / len(shards), top_value / len(shards))
        level = level * jnp.repeat(jnp.exp(heights), shape[axis_at] // blocks).reshape((-1,) + (1,) * (len(shape) - 1 - axis_at))
    return level


def scatter_about(key, shape, deviation, reach, split=(), held_as=jnp.bfloat16):
    loudness = level_of(key, shape, split, -0.22, 0.18) if split else 1.0
    values = jax.random.normal(key, shape, jnp.float32) * deviation * loudness
    return jnp.minimum(jnp.maximum(values, -reach), reach).astype(held_as)


def setup_inputs(seed: int = 0) -> dict:
    arg_keys = jax.random.split(jax.random.key(seed), 6)
    inputs = scatter_about(arg_keys[0], (TOKENS, D), 1.0, 6.0, ((0, 8), (1, 4)))
    out_grad = scatter_about(arg_keys[1], (TOKENS, D), (TOKENS ** -0.25), 2.0, ((0, 8), (1, 4)))
    w_gate = scatter_about(arg_keys[2], (D, FF), D ** -0.5, 0.0546875, ((0, 4), (1, 32)))
    w_up = scatter_about(arg_keys[3], (D, FF), D ** -0.5, 0.0546875, ((0, 4), (1, 32)))
    w_down = scatter_about(arg_keys[4], (FF, D), FF ** -0.5, 0.09375, ((0, 4), (1, 32)))
    return {"inputs": inputs, "out_grad": out_grad, "w_gate": w_gate, "w_up": w_up, "w_down": w_down}


def reference(inputs, out_grad, w_gate, w_up, w_down):
    gate = jnp.dot(inputs, w_gate, preferred_element_type=jnp.float32)
    up = jnp.dot(inputs, w_up, preferred_element_type=jnp.float32)
    back = jnp.dot(out_grad, w_down.T, preferred_element_type=jnp.float32)
    sig = jax.nn.sigmoid(gate)
    act = gate * sig
    hidden = (act * up).astype(jnp.bfloat16)
    d_gate = (back * up * sig * (1.0 + gate * (1.0 - sig))).astype(jnp.bfloat16)
    d_up = (back * act).astype(jnp.bfloat16)
    d_inputs = jnp.dot(d_gate, w_gate.T, preferred_element_type=jnp.float32) + jnp.dot(d_up, w_up.T, preferred_element_type=jnp.float32)
    grad_gate = jnp.dot(inputs.T, d_gate, preferred_element_type=jnp.float32)
    grad_up = jnp.dot(inputs.T, d_up, preferred_element_type=jnp.float32)
    grad_down = jnp.dot(hidden.T, out_grad, preferred_element_type=jnp.float32)
    return d_inputs.astype(jnp.bfloat16), grad_gate.astype(jnp.bfloat16), grad_up.astype(jnp.bfloat16), grad_down.astype(jnp.bfloat16)
```

```python
import jax
import jax.numpy as jnp
from jax import lax
from jax.experimental import pallas as pl
from jax.experimental.pallas import tpu as pltpu
from jax.sharding import PartitionSpec as P

MESH = pl.DeviceIdType.MESH
F32 = jnp.float32
BF16 = jnp.bfloat16
N_SEM = 168
ORDER = (0, 1, 3, 2)


def kernel(
    inputs, out_grad, w_gate, w_up, w_down,
    d_in, g_gate, g_up, g_down,
    xin, wcat, og, wdn, pbuf, pr, s2, xr, yr, zg, zgr, zb, zbr, dcat, hid, dxs, dx0, dxr, dxzr, gs,
    ssem, rsem, lsem,
):
    i = lax.axis_index("in")
    x = lax.axis_index("out")
    t = lax.axis_index("tok")
    h, c, y, l = i // 2, i % 2, t // 2, t % 2
    z = 2 * h + l

    def dev(dx=0, dy=0, dz=0, dc=0):
        zz = (z + dz) % 4
        return (2 * (zz // 2) + (c + dc) % 2, (x + dx) % 4, 2 * ((y + dy) % 4) + zz % 2)

    def lpart():
        return (i, x, 2 * y + 1 - l)

    def al(v, n):
        return pl.multiple_of(v, n)

    index, sent, local = {}, [], []

    def sem_of(key):
        if key not in index:
            index[key] = len(index)
        return index[key]

    def send(key, src, dst, device):
        n = sem_of(key)
        copy = pltpu.make_async_remote_copy(
            src_ref=src, dst_ref=dst, send_sem=ssem.at[n], recv_sem=rsem.at[n],
            device_id=device, device_id_type=MESH,
        )
        copy.start()
        sent.append(copy)
        return copy

    def recv(key, dst):
        n = sem_of(key)
        pltpu.make_async_remote_copy(
            src_ref=dst, dst_ref=dst, send_sem=ssem.at[n], recv_sem=rsem.at[n],
            device_id=dev(dc=1), device_id_type=MESH,
        ).wait_recv()

    def move(src, dst):
        copy = pltpu.make_async_copy(src, dst, lsem.at[len(local)])
        copy.start()
        local.append(copy)
        return copy

    own_in = move(inputs.at[:, pl.ds(al(x * 768, 128), 768)], xin.at[pl.ds(al(l * 256, 256), 256), :])
    own_og = move(out_grad.at[:, pl.ds(al(t * 384, 128), 384)], og.at[pl.ds(al(l * 256, 256), 256), :])
    own_dn = move(w_down, wdn)
    own_w = [
        move(w.at[pl.ds(al(x * 768, 256), 768), :], wcat.at[:, pl.ds(128 * q, 128)])
        for q, w in enumerate((w_gate, w_up))
    ]

    barrier = pltpu.get_barrier_semaphore()
    peers = [dev(dc=1)]
    peers += [dev(dx=m) for m in (1, 2, 3)]
    peers += [dev(dy=m) for m in (1, 2, 3)]
    peers += [dev(dz=m) for m in (1, 2, 3)]
    cross = [(i, x, 2 * ((y + m) % 4) + 1 - l) for m in (1, 2, 3)]
    peers += cross
    for peer in peers:
        pl.semaphore_signal(barrier, inc=1, device_id=peer, device_id_type=MESH)
    pl.semaphore_wait(barrier, len(peers))

    def own_rows(m, part):
        return pl.ds(al(((4 - m) % 4) * 512 + part * 256, 256), 256)

    send(("og", 0, 1), out_grad.at[:, pl.ds(al((2 * y + 1 - l) * 384, 128), 384)], og.at[own_rows(0, l), :], lpart())
    send(
        ("in", 0, 1), inputs.at[:, pl.ds(al(x * 768, 128), 768)],
        xin.at[own_rows(0, l), :], lpart(),
    )
    for m in (2, 1, 3):
        there = (y + m) % 4
        send(("og", m, 0), out_grad.at[:, pl.ds(al((2 * there + l) * 384, 128), 384)], og.at[own_rows(m, l), :], dev(dy=m))
        send(("og", m, 1), out_grad.at[:, pl.ds(al((2 * there + 1 - l) * 384, 128), 384)], og.at[own_rows(m, l), :], cross[m - 1])
    for j in (2, 1, 3):
        for q, w in enumerate((w_gate, w_up)):
            send(
                ("w", j, q), w.at[pl.ds(al(((x + j) % 4) * 768, 256), 768), :],
                wcat.at[:, pl.ds(256 * (4 - j) + 128 * q, 128)], dev(dx=j),
            )
    own_in.wait()
    for m in (1, 3, 2):
        send(("in", m, 0), xin.at[pl.ds(al(l * 256, 256), 256), :], xin.at[own_rows(m, l), :], dev(dy=m))
    recv(("in", 0, 1), xin.at[pl.ds(al((1 - l) * 256, 256), 256), :])
    for m in (1, 3, 2):
        send(("in", m, 1), xin.at[pl.ds(al((1 - l) * 256, 256), 256), :], xin.at[own_rows(m, 1 - l), :], dev(dy=m))

    for copy in [own_og, own_dn] + own_w:
        copy.wait()

    def rows(k, part=0):
        return pl.ds(al(k * 512 + part * 256, 256), 256)

    uses = []

    def partial_slot():
        n = len(uses)
        if n >= 2:
            uses[n - 2].wait_send()
        return n % 2

    def core_reduce_start(key, slot, n):
        uses.append(send((key, n), pbuf.at[slot, pl.ds(al((1 - c) * 256, 256), 256), :], pr.at[n], dev(dc=1)))

    slots = {}

    def b1(k):
        if k:
            recv(("og", 4 - k, 0), og.at[rows(k, l), :])
            recv(("og", 4 - k, 1), og.at[rows(k, 1 - l), :])
        else:
            recv(("og", 0, 1), og.at[rows(0, 1 - l), :])
        slot = partial_slot()
        slots["b", k] = slot

        @pl.loop(0, 4)
        def _(m):
            there = (y + m) % 4
            pbuf[slot, :, pl.ds(al(m * 256, 256), 256)] = lax.dot_general(
                og[pl.ds(512 * k, 512), :], wdn[pl.ds(al(there * 256, 256), 256), :],
                (((1,), (1,)), ((), ())), preferred_element_type=F32,
            )

        core_reduce_start("cr", slot, 4 + k)

    def core_sum(slot, n):
        recv(("cr", n), pr.at[n])

        @pl.loop(0, 8)
        def _(r):
            at = pl.ds(al(r * 32, 32), 32)
            mine = pl.ds(al(c * 256 + r * 32, 32), 32)
            total = pbuf[slot, mine, :] + pr[n, at, :]
            pr[n, at, :] = total
            s2[n, at, :] = total.astype(BF16)

    def b2(k):
        core_sum(slots["b", k], 4 + k)
        for m in (2, 1, 3):
            send(("yr", (k - m) % 4, m), s2.at[4 + k, :, pl.ds(256 * m, 256)], yr.at[(k - m) % 4, m - 1], dev(dy=m))

    def g1(k):
        if k:
            recv(("in", 4 - k, 0), xin.at[rows(k, l), :])
            recv(("in", 4 - k, 1), xin.at[rows(k, 1 - l), :])
        slot = partial_slot()
        slots["g", k] = slot

        @pl.loop(0, 4)
        def _(n):
            at = pl.ds(al(n * 256, 256), 256)
            pbuf[slot, :, at] = jnp.dot(xin[pl.ds(512 * k, 512), :], wcat[:, at], preferred_element_type=F32)

        core_reduce_start("cr", slot, k)

    def g2(k):
        core_sum(slots["g", k], k)
        for j in (2, 1, 3):
            send(("xr", k, j), s2.at[k, :, pl.ds(256 * j, 256)], xr.at[k, j - 1], dev(dx=j))

    def b3(k):
        for m in (1, 2, 3):
            recv(("yr", k, m), yr.at[k, m - 1])
        zb[k] = (pr[4 + k, :, 0:256] + yr[k, 0].astype(F32)) + (yr[k, 1].astype(F32) + yr[k, 2].astype(F32))
        for d in (2, 1, 3):
            zz = (z + d) % 4
            send(
                ("zb", k, d), zb.at[k, pl.ds(al((zz // 2) * 128, 128), 128), pl.ds(al((zz % 2) * 128, 128), 128)],
                zbr.at[k, d - 1], dev(dz=d),
            )

    def g3(k):
        for j in (1, 2, 3):
            recv(("xr", k, j), xr.at[k, j - 1])
        zg[k] = (pr[k, :, 0:256] + xr[k, 0].astype(F32)) + (xr[k, 1].astype(F32) + xr[k, 2].astype(F32))
        send(("zg", k), zg.at[k, pl.ds(al((1 - h) * 128, 128), 128), :], zgr.at[k], dev(dz=2))

    def e(k):
        recv(("zg", k), zgr.at[k])
        for d in (1, 2, 3):
            recv(("zb", k, d), zbr.at[k, d - 1])
        mine = pl.ds(al(h * 128, 128), 128)
        both = zg[k, mine, :] + zgr[k]
        gate, up = both[:, :128], both[:, 128:]
        back = (zb[k, mine, pl.ds(al(l * 128, 128), 128)] + zbr[k, 0]) + (zbr[k, 1] + zbr[k, 2])
        sig = jax.nn.sigmoid(gate)
        act = gate * sig
        at = pl.ds(al(k * 512 + c * 256 + h * 128, 128), 128)
        dcat[at, 0:128] = (back * up * sig * (1.0 + gate * (1.0 - sig))).astype(BF16)
        dcat[at, 128:256] = (back * act).astype(BF16)
        cols = pl.ds(al(l * 128, 128), 128)
        hid[at, cols] = (act * up).astype(BF16)
        send(("ag", k), dcat.at[at, 0:256], dcat.at[at, 0:256], dev(dz=2))
        for d in (2, 1, 3):
            send(("ah", k, d), hid.at[at, cols], hid.at[at, cols], dev(dz=d))

    def half(k, part):
        return pl.ds(al(k * 512 + part * 256, 256), 256)

    def a2(k):
        there = pl.ds(al(k * 512 + c * 256 + (1 - h) * 128, 128), 128)
        recv(("ag", k), dcat.at[there, 0:256])
        for j in (2, 1, 3):
            send(("xg", k, j), dcat.at[half(k, c), 0:256], dcat.at[half(k, c), pl.ds(256 * (4 - j), 256)], dev(dx=j))
        for d in (1, 2, 3):
            zz = (z - d + 4) % 4
            at = pl.ds(al(k * 512 + c * 256 + (zz // 2) * 128, 128), 128)
            recv(("ah", k, d), hid.at[at, pl.ds(al((zz % 2) * 128, 128), 128)])
        for m in (2, 1, 3):
            kk = (k - m) % 4
            send(("yg", kk, m), hid.at[half(k, c), 0:256], hid.at[half(kk, c), pl.ds(256 * (4 - m), 256)], dev(dy=m))

    def a3(k):
        for j in (1, 2, 3):
            recv(("xg", k, j), dcat.at[half(k, c), pl.ds(256 * (4 - j), 256)])
        send(("cg", k), dcat.at[half(k, c), :], dcat.at[half(k, c), :], dev(dc=1))

    def xk(k):
        recv(("cg", k), dcat.at[half(k, 1 - c), :])

        @pl.loop(0, 3)
        def _(n):
            at = pl.ds(al(n * 256, 256), 256)
            part = lax.dot_general(
                dcat[pl.ds(512 * k, 512), :], wcat[at, :], (((1,), (1,)), ((), ())), preferred_element_type=F32
            )
            if k:
                dxs[k - 1, :, at] = part.astype(BF16)
            else:
                dx0[:, at] = part

        if k:
            send(("dx", k), dxs.at[k - 1], dxr.at[k - 1], dev(dy=k))

    def a4(k):
        for m in (1, 2, 3):
            recv(("yg", k, m), hid.at[half(k, c), pl.ds(256 * (4 - m), 256)])
        send(("ch", k), hid.at[half(k, c), :], hid.at[half(k, c), :], dev(dc=1))

    o = ORDER
    b1(o[0])
    b1(o[1])
    b2(o[0])
    b1(o[2])
    b2(o[1])
    b1(o[3])
    b2(o[2])
    for j in (1, 2, 3):
        for q in (0, 1):
            recv(("w", j, q), wcat.at[:, pl.ds(256 * (4 - j) + 128 * q, 128)])

    def g3b3(k):
        g3(k)
        b3(k)

    stages = (g1, g2, g3b3, e, a2, a3, xk)
    for step in range(len(stages) + 3):
        for s in reversed(range(len(stages))):
            if 0 <= step - s < 4:
                stages[s](o[step - s])
        if step == 0:
            b2(o[3])

    def grad_slot(j):
        @pl.loop(0, 3)
        def _(n):
            at = pl.ds(al(n * 256, 256), 256)
            gs[j, at, :] = lax.dot_general(
                xin[:, at], dcat[:, 256 * j : 256 * j + 256], (((0,), (0,)), ((), ())), preferred_element_type=F32
            ).astype(BF16)

        here = pl.ds(al(x * 768, 256), 768)
        for q, out in enumerate((g_gate, g_up)):
            src = gs.at[j, :, pl.ds(128 * q, 128)]
            if j:
                send(("gw", j, q), src, out.at[here, :], dev(dx=j))
            else:
                move(src, out.at[here, :])

    for j in (2, 1, 3, 0):
        grad_slot(j)

    for k in o:
        a4(k)
    for k in range(4):
        recv(("ch", k), hid.at[half(k, 1 - c), :])

    @pl.loop(0, 4)
    def _(m):
        there = (y + m) % 4
        g_down[pl.ds(al(there * 256, 256), 256), :] = lax.dot_general(
            hid[:, pl.ds(al(m * 256, 256), 256)], og[...], (((0,), (0,)), ((), ())), preferred_element_type=F32
        ).astype(BF16)

    for k in (1, 2, 3):
        recv(("dx", k), dxr.at[k - 1])

    @pl.loop(0, 16)
    def _(r):
        at = pl.ds(al(r * 32, 32), 32)
        dx0[at, :] = (dx0[at, :] + dxr[0, at, :].astype(F32)) + (dxr[1, at, :].astype(F32) + dxr[2, at, :].astype(F32))

    send(("dz",), dx0.at[pl.ds(al((1 - l) * 256, 256), 256), :], dxzr, lpart())
    recv(("dz",), dxzr)

    @pl.loop(0, 8)
    def _(r):
        at = pl.ds(al(r * 32, 32), 32)
        d_in[at, :] = (dx0[pl.ds(al(l * 256 + r * 32, 32), 32), :] + dxzr[at, :]).astype(BF16)

    for j in (1, 2, 3):
        for q, out in enumerate((g_gate, g_up)):
            recv(("gw", j, q), out.at[pl.ds(al(((x - j + 4) % 4) * 768, 256), 768), :])
    for copy in local[5:]:
        copy.wait()
    done = [id(copy) for copy in uses[:-2]]
    for copy in sent:
        if id(copy) not in done:
            copy.wait_send()
    assert len(index) <= N_SEM, len(index)


def shards(inputs, out_grad, w_gate, w_up, w_down):
    v = pltpu.VMEM
    any_ = pl.BlockSpec(memory_space=pl.ANY)
    vm = pl.BlockSpec(memory_space=pltpu.VMEM)
    return pl.pallas_call(
        kernel,
        name="swiglu_back",
        out_shape=(
            jax.ShapeDtypeStruct((256, 768), BF16),
            jax.ShapeDtypeStruct((3072, 128), BF16),
            jax.ShapeDtypeStruct((3072, 128), BF16),
            jax.ShapeDtypeStruct((1024, 384), BF16),
        ),
        in_specs=[any_] * 5,
        out_specs=(vm, any_, any_, vm),
        scratch_shapes=[
            v((2048, 768), BF16),
            v((768, 1024), BF16),
            v((2048, 384), BF16),
            v((1024, 384), BF16),
            v((2, 512, 1024), F32),
            v((8, 256, 1024), F32),
            v((8, 256, 1024), BF16),
            v((4, 3, 256, 256), BF16),
            v((4, 3, 256, 256), BF16),
            v((4, 256, 256), F32),
            v((4, 128, 256), F32),
            v((4, 256, 256), F32),
            v((4, 3, 128, 128), F32),
            v((2048, 1024), BF16),
            v((2048, 1024), BF16),
            v((3, 512, 768), BF16),
            v((512, 768), F32),
            v((3, 512, 768), BF16),
            v((256, 768), F32),
            v((4, 768, 256), BF16),
            pltpu.SemaphoreType.DMA((N_SEM,)),
            pltpu.SemaphoreType.DMA((N_SEM,)),
            pltpu.SemaphoreType.DMA((8,)),
        ],
        compiler_params=pltpu.CompilerParams(collective_id=0, has_side_effects=True, vmem_limit_bytes=60 * 2**20),
        cost_estimate=pl.CostEstimate(flops=13 * 10**9, bytes_accessed=8 * 2**20, transcendentals=65536),
    )(inputs, out_grad, w_gate, w_up, w_down)


def solution(mesh):
    in_specs = (
        P("tok", "in"),
        P("tok", "in"),
        P("in", ("out", "tok")),
        P("in", ("out", "tok")),
        P("out", ("in", "tok")),
    )
    out_specs = (
        P("tok", ("in", "out")),
        P("in", ("out", "tok")),
        P("in", ("out", "tok")),
        P("out", ("in", "tok")),
    )
    return jax.shard_map(shards, mesh=mesh, in_specs=in_specs, out_specs=out_specs, check_vma=False)
```

```python
import jax
import jax.numpy as jnp
from jax import lax
from jax.experimental import pallas as pl
from jax.experimental.pallas import tpu as pltpu
from jax.sharding import PartitionSpec as P

MESH = pl.DeviceIdType.MESH
F32 = jnp.float32
BF16 = jnp.bfloat16
N_SEM = 230
N_SLOT = 3
DZ = (0, 2)
DY = tuple(k for k in range(4) if k not in DZ)
Z_FIRST = (0, 1, 2, 3)
FWD_IN, FWD_XG, FWD_YG, FWD_OG = True, False, True, False


def kernel(
    inputs, out_grad, w_gate, w_up, w_down,
    d_in, g_gate, g_up, g_down,
    xin, wcat, og, wdn, pbuf, pr, s2, xr, yr, zg, zgr, zb, zbr, dcat, hid, dzs, dzr, dxo, dxf, dxs, dxr, gs, gacc,
    ssem, rsem, lsem,
):
    i = lax.axis_index("in")
    x = lax.axis_index("out")
    t = lax.axis_index("tok")
    h, c, y, l = i // 2, i % 2, t // 2, t % 2
    z = 2 * h + l

    def dev(dx=0, dy=0, dz=0, dc=0):
        zz = (z + dz) % 4
        return (2 * (zz // 2) + (c + dc) % 2, (x + dx) % 4, 2 * ((y + dy) % 4) + zz % 2)

    def lpart():
        return (i, x, 2 * y + 1 - l)

    def al(v, n):
        return pl.multiple_of(v, n)

    index, sent, local, got = {}, [], [], set()

    def sem_of(key):
        if key not in index:
            index[key] = len(index)
        return index[key]

    def send(key, src, dst, device):
        n = sem_of(key)
        copy = pltpu.make_async_remote_copy(
            src_ref=src, dst_ref=dst, send_sem=ssem.at[n], recv_sem=rsem.at[n],
            device_id=device, device_id_type=MESH,
        )
        copy.start()
        sent.append(copy)
        return copy

    def recv(key, dst):
        if key in got:
            return
        got.add(key)
        n = sem_of(key)
        pltpu.make_async_remote_copy(
            src_ref=dst, dst_ref=dst, send_sem=ssem.at[n], recv_sem=rsem.at[n],
            device_id=dev(dc=1), device_id_type=MESH,
        ).wait_recv()

    def move(src, dst):
        copy = pltpu.make_async_copy(src, dst, lsem.at[len(local)])
        copy.start()
        local.append(copy)
        return copy

    def rows(s, yy, ll):
        return pl.ds(al(s * 512 + ll * 256 + yy * 64, 64), 64)

    def half(s, part):
        return pl.ds(al(s * 512 + part * 256, 256), 256)

    cols_in = pl.ds(al(x * 768, 128), 768)
    mine16 = pl.ds(al(x * 16, 16), 16)
    own_in = []
    for s in range(4):
        here = pl.ds(64 * s, 64)
        own_in.append(move(inputs.at[here, cols_in], xin.at[rows(s, y, l), :]))
    own_og = move(out_grad.at[:, x, :, pl.ds(al(t * 384, 128), 384)], og.at[:, 4 * l + y, mine16, :])
    own_dn = move(w_down, wdn)
    own_w = [
        move(w.at[pl.ds(al(x * 768, 256), 768), :], wcat.at[:, pl.ds(128 * q, 128)])
        for q, w in enumerate((w_gate, w_up))
    ]
    n_first = len(local)

    barrier = pltpu.get_barrier_semaphore()
    peers = [dev(dc=1)]
    peers += [dev(dx=m) for m in (1, 2, 3)]
    peers += [dev(dy=m) for m in (1, 2, 3)]
    peers += [dev(dz=m) for m in (1, 2, 3)]
    cross = [(i, x, 2 * ((y + m) % 4) + 1 - l) for m in (1, 2, 3)]
    peers += cross
    for peer in peers:
        pl.semaphore_signal(barrier, inc=1, device_id=peer, device_id_type=MESH)
    pl.semaphore_wait(barrier, len(peers))

    def og_cols(yy, ll):
        return pl.ds(al((2 * yy + ll) * 384, 128), 384)

    def st_og():
        send(("og", 0, 1), out_grad.at[:, x, :, og_cols(y, 1 - l)], og.at[:, 4 * l + y, mine16, :], lpart())
        for m in (2, 1, 3):
            there = (y + m) % 4
            send(("og", m, 0), out_grad.at[:, x, :, og_cols(there, l)], og.at[:, 4 * l + y, mine16, :], dev(dy=m))
            send(("og", m, 1), out_grad.at[:, x, :, og_cols(there, 1 - l)], og.at[:, 4 * l + y, mine16, :], cross[m - 1])

    def take_og():
        own_og.wait()
        recv(("og", 0, 1), og.at[:, 4 * (1 - l) + y, mine16, :])
        for m in (1, 3, 2):
            yy = (y - m + 4) % 4
            recv(("og", m, 0), og.at[:, 4 * l + yy, mine16, :])
            recv(("og", m, 1), og.at[:, 4 * (1 - l) + yy, mine16, :])

    def og_part(s, j, lo=0, n=16):
        return og.at[s, :, pl.ds(al(((x + j) % 4) * 16 + lo, n), n), :]

    def ox(s):
        if s == 0:
            take_og()
        for j in (1, 3) if FWD_OG else (2, 1, 3):
            send(("ox", s, j), og_part(s, 0), og_part(s, 0), dev(dx=j))

    def fo(s):
        if FWD_OG:
            for j in (1, 3):
                part = og.at[s, pl.ds(0 if j == 1 else 4, 4), pl.ds(al(((x - j + 4) % 4) * 16, 16), 16), :]
                recv(("ox", s, j), og_part(s, 4 - j))
                send(("of", s, j), part, part, dev(dx=j))

    def wait_og(s):
        if FWD_OG:
            for j in (1, 3):
                recv(("of", s, j), og.at[s, pl.ds(0 if j == 1 else 4, 4), pl.ds(al(((x + 2) % 4) * 16, 16), 16), :])
        else:
            for j in (1, 3, 2):
                recv(("ox", s, j), og_part(s, 4 - j))

    def stz(s):
        here = pl.ds(64 * s, 64)
        at = rows(s, y, l)
        send(("in", s, 0, 1), inputs.at[here, cols_in], xin.at[at, :], lpart())

    def sty(s):
        here = pl.ds(64 * s, 64)
        at = rows(s, y, l)
        for m in (1, 3) if FWD_IN else (2, 1, 3):
            send(("in", s, m, 0), inputs.at[here, cols_in], xin.at[at, :], dev(dy=m))

    def st_w(q):
        w = (w_gate, w_up)[q]
        for j in (2, 1, 3):
            send(
                ("w", j, q), w.at[pl.ds(al(((x + j) % 4) * 768, 256), 768), :],
                wcat.at[:, pl.ds(256 * (4 - j) + 128 * q, 128)], dev(dx=j),
            )

    def part_rows(s, yy, ll, m):
        return pl.ds(al(s * 512 + ll * 256 + yy * 64 + (0 if m == 1 else 32), 32), 32)

    def fw(s):
        if s in Z_FIRST:
            at = rows(s, y, 1 - l)
            recv(("in", s, 0, 1), xin.at[at, :])
            for m in (1, 3) if FWD_IN else (2, 1, 3):
                send(("in", s, m, 1), xin.at[at, :], xin.at[at, :], dev(dy=m))

    def fi(s):
        if FWD_IN:
            for q in (0, 1) if s in Z_FIRST else (0,):
                for m in (1, 3):
                    yy, ll = (y - m + 4) % 4, (1 - l if q else l)
                    recv(("in", s, m, q), xin.at[rows(s, yy, ll), :])
                    at = part_rows(s, yy, ll, m)
                    send(("if", s, m, q), xin.at[at, :], xin.at[at, :], dev(dy=m))

    def far_in(s, q):
        yy, ll = (y + 2) % 4, (1 - l if q else l)
        if FWD_IN:
            for m in (1, 3):
                recv(("if", s, m, q), xin.at[part_rows(s, yy, ll, m), :])
        else:
            recv(("in", s, 2, q), xin.at[rows(s, yy, ll), :])

    def fz(s):
        if s not in Z_FIRST:
            for m in (1, 3, 2):
                at = rows(s, (y - m + 4) % 4, l)
                if m == 2:
                    far_in(s, 0)
                elif not FWD_IN:
                    recv(("in", s, m, 0), xin.at[at, :])
                send(("in", s, m, 1), xin.at[at, :], xin.at[at, :], lpart())

    def wait_in(s):
        own_in[s].wait()
        if s in Z_FIRST:
            if not FWD_IN:
                for m in (1, 3):
                    for q in (0, 1):
                        recv(("in", s, m, q), xin.at[rows(s, (y - m + 4) % 4, 1 - l if q else l), :])
            far_in(s, 0)
            far_in(s, 1)
        else:
            recv(("in", s, 0, 1), xin.at[rows(s, y, 1 - l), :])
            for m in (1, 3, 2):
                recv(("in", s, m, 1), xin.at[rows(s, (y - m + 4) % 4, 1 - l), :])

    uses = []

    def partial_slot():
        n = len(uses)
        if n >= N_SLOT:
            uses[n - N_SLOT].wait_send()
        return n % N_SLOT

    def core_send(slot, n):
        uses.append(send(("cr", n), pbuf.at[slot, pl.ds(al((1 - c) * 256, 256), 256), :], pr.at[n], dev(dc=1)))

    slots, seen = {}, []

    def b1(s):
        wait_og(s)
        if s == 0:
            own_dn.wait()
        slot = partial_slot()
        slots["b", s] = slot

        @pl.loop(0, 4)
        def _(m):
            there = (y + m) % 4
            pbuf[slot, :, pl.ds(al(m * 256, 256), 256)] = lax.dot_general(
                og[s].reshape(512, 384), wdn[pl.ds(al(there * 256, 256), 256), :],
                (((1,), (1,)), ((), ())), preferred_element_type=F32,
            )

        core_send(slot, 4 + s)

    def g1(s):
        wait_in(s)
        if s == 0:
            for copy in own_w:
                copy.wait()
            for j in (1, 3, 2):
                for q in (0, 1):
                    recv(("w", j, q), wcat.at[:, pl.ds(256 * (4 - j) + 128 * q, 128)])
        slot = partial_slot()
        slots["g", s] = slot

        @pl.loop(0, 4)
        def _(n):
            at = pl.ds(al(n * 256, 256), 256)
            pbuf[slot, :, at] = jnp.dot(xin[pl.ds(512 * s, 512), :], wcat[:, at], preferred_element_type=F32)

        core_send(slot, s)

    def core_sum(slot, n):
        recv(("cr", n), pr.at[n])

        @pl.loop(0, 8)
        def _(r):
            at = pl.ds(al(r * 32, 32), 32)
            mine = pl.ds(al(c * 256 + r * 32, 32), 32)
            total = pbuf[slot, mine, :] + pr[n, at, :]
            pr[n, at, :] = total
            s2[n, at, :] = total.astype(BF16)

    def b2(s):
        core_sum(slots["b", s], 4 + s)
        for m in (2, 1, 3):
            send(("yr", s, m), s2.at[4 + s, :, pl.ds(256 * m, 256)], yr.at[s, m - 1], dev(dy=m))

    def g2(s):
        core_sum(slots["g", s], s)
        for j in (2, 1, 3):
            send(("xr", s, j), s2.at[s, :, pl.ds(256 * j, 256)], xr.at[s, j - 1], dev(dx=j))

    def b3(k):
        for m in (1, 3, 2):
            recv(("yr", k, m), yr.at[k, m - 1])
        zb[k] = (pr[4 + k, :, 0:256] + yr[k, 0].astype(F32)) + (yr[k, 1].astype(F32) + yr[k, 2].astype(F32))
        for d in (2, 1, 3):
            zz = (z + d) % 4
            send(
                ("zb", k, d), zb.at[k, pl.ds(al((zz // 2) * 128, 128), 128), pl.ds(al((zz % 2) * 128, 128), 128)],
                zbr.at[k, d - 1], dev(dz=d),
            )

    def g3(k):
        for j in (1, 3, 2):
            recv(("xr", k, j), xr.at[k, j - 1])
        zg[k] = (pr[k, :, 0:256] + xr[k, 0].astype(F32)) + (xr[k, 1].astype(F32) + xr[k, 2].astype(F32))
        send(("zg", k), zg.at[k, pl.ds(al((1 - h) * 128, 128), 128), :], zgr.at[k], dev(dz=2))

    def e(k):
        recv(("zg", k), zgr.at[k])
        for d in (1, 2, 3):
            recv(("zb", k, d), zbr.at[k, d - 1])
        mine = pl.ds(al(h * 128, 128), 128)
        both = zg[k, mine, :] + zgr[k]
        gate, up = both[:, :128], both[:, 128:]
        back = (zb[k, mine, pl.ds(al(l * 128, 128), 128)] + zbr[k, 0]) + (zbr[k, 1] + zbr[k, 2])
        sig = jax.nn.sigmoid(gate)
        act = gate * sig
        at = pl.ds(al(k * 512 + c * 256 + h * 128, 128), 128)
        dcat[at, 0:128] = (back * up * sig * (1.0 + gate * (1.0 - sig))).astype(BF16)
        dcat[at, 128:256] = (back * act).astype(BF16)
        cols = pl.ds(al(l * 128, 128), 128)
        hid[at, cols] = (act * up).astype(BF16)
        send(("ag", k), dcat.at[at, 0:256], dcat.at[at, 0:256], dev(dz=2))
        for d in (2, 1, 3):
            send(("ah", k, d), hid.at[at, cols], hid.at[at, cols], dev(dz=d))

    def a2x(k):
        there = pl.ds(al(k * 512 + c * 256 + (1 - h) * 128, 128), 128)
        recv(("ag", k), dcat.at[there, 0:256])
        for j in (1, 3) if FWD_XG else (2, 1, 3):
            send(("xg", k, j), dcat.at[half(k, c), 0:256], dcat.at[half(k, c), pl.ds(256 * (4 - j), 256)], dev(dx=j))

    def a2y(k):
        for d in (1, 2, 3):
            zz = (z - d + 4) % 4
            at = pl.ds(al(k * 512 + c * 256 + (zz // 2) * 128, 128), 128)
            recv(("ah", k, d), hid.at[at, pl.ds(al((zz % 2) * 128, 128), 128)])
        for m in (1, 3) if FWD_YG else (2, 1, 3):
            send(("yg", k, m), hid.at[half(k, c), 0:256], hid.at[half(k, c), pl.ds(256 * (4 - m), 256)], dev(dy=m))

    def fwd_half(k, j):
        return pl.ds(al(k * 512 + c * 256 + (0 if j == 1 else 128), 128), 128)

    def af(k, on, name, buf, to):
        if on:
            for j in (1, 3):
                recv((name, k, j), buf.at[half(k, c), pl.ds(256 * (4 - j), 256)])
                send((name + "f", k, j), buf.at[fwd_half(k, j), pl.ds(256 * (4 - j), 256)], buf.at[fwd_half(k, j), pl.ds(512, 256)], to(j))

    def afx(k):
        af(k, FWD_XG, "xg", dcat, lambda j: dev(dx=j))

    def afy(k):
        af(k, FWD_YG, "yg", hid, lambda j: dev(dy=j))

    def gathered(k, on, name, buf):
        if on:
            for j in (1, 3):
                recv((name + "f", k, j), buf.at[fwd_half(k, j), pl.ds(512, 256)])
        else:
            for j in (1, 3, 2):
                recv((name, k, j), buf.at[half(k, c), pl.ds(256 * (4 - j), 256)])

    def a3(k):
        gathered(k, FWD_XG, "xg", dcat)
        send(("cg", k), dcat.at[half(k, c), :], dcat.at[half(k, c), :], dev(dc=1))

    def a4(k):
        gathered(k, FWD_YG, "yg", hid)
        send(("ch", k), hid.at[half(k, c), :], hid.at[half(k, c), :], dev(dc=1))

    def need_d(k):
        recv(("cg", k), dcat.at[half(k, 1 - c), :])

    def times_w(lhs, n):
        return lax.dot_general(
            lhs, wcat[pl.ds(al(n * 256, 256), 256), :], (((1,), (1,)), ((), ())), preferred_element_type=F32
        )

    def xk(k):
        need_d(k)
        if k in DZ:
            n_k = DZ.index(k)

            @pl.loop(0, 3)
            def _(n):
                at = pl.ds(al(n * 256, 256), 256)
                part = times_w(jnp.concatenate([dcat[half(k, 1 - l), :], dcat[half(k, l), :]], axis=0), n)
                dzs[k, :, at] = part[:256].astype(BF16)
                dxo[n_k, :, at] = part[256:]

            send(("dz", k), dzs.at[k], dzr.at[k], lpart())
        else:
            n_k = DY.index(k)

            @pl.loop(0, 3)
            def _(n):
                at = pl.ds(al(n * 256, 256), 256)
                part = times_w(dcat[pl.ds(512 * k, 512), :], n).reshape(2, 4, 64, 256)
                dxs[k, :, :, :, at] = part.astype(BF16)
                dxf[n_k, :, :, :, at] = part

            for m in (2, 1, 3):
                send(("dx", k, m), dxs.at[k, :, (y + m) % 4], dxr.at[k, m - 1], dev(dy=m))

    def x2(k):
        if k in DZ:
            n_k = DZ.index(k)
            recv(("dz", k), dzr.at[k])

            @pl.loop(0, 4)
            def _(r):
                at = pl.ds(al(r * 64, 64), 64)
                total = dxo[n_k, at, :] + dzr[k, at, :].astype(F32)
                dxo[n_k, at, :] = total
                dxs[k, 0, r] = total.astype(BF16)

            for m in (2, 1, 3):
                send(("dx", k, m), dxs.at[k, 0, (y + m) % 4], dxr.at[k, m - 1, 0], dev(dy=m))
        else:
            n_k = DY.index(k)
            for m in (1, 3, 2):
                recv(("dx", k, m), dxr.at[k, m - 1])
            total = (dxf[n_k, :, y] + dxr[k, 0].astype(F32)) + (dxr[k, 1].astype(F32) + dxr[k, 2].astype(F32))
            dxf[n_k, :, 0] = total
            dxs[k, :, y] = total.astype(BF16)
            send(("dz", k), dxs.at[k, 1 - l, y], dzr.at[k, 0:64], lpart())

    def xt(k):
        at = pl.ds(64 * k, 64)
        if k in DZ:
            for m in (1, 3, 2):
                recv(("dx", k, m), dxr.at[k, m - 1, 0])
            d_in[at, :] = (
                (dxo[DZ.index(k), pl.ds(al(y * 64, 64), 64), :] + dxr[k, 0, 0].astype(F32))
                + (dxr[k, 1, 0].astype(F32) + dxr[k, 2, 0].astype(F32))
            ).astype(BF16)
        else:
            recv(("dz", k), dzr.at[k, 0:64])
            d_in[at, :] = (dxf[DY.index(k), l, 0] + dzr[k, 0:64].astype(F32)).astype(BF16)

    def grad_part(k, n, cols):
        at = pl.ds(al(n * 256, 256), 256)
        return at, lax.dot_general(
            xin[pl.ds(512 * k, 512), at], dcat[pl.ds(512 * k, 512), cols], (((0,), (0,)), ((), ())),
            preferred_element_type=F32,
        )

    begun = []

    def gp(k):
        need_d(k)
        first = not begun
        begun.append(k)

        @pl.loop(0, 3)
        def _(n):
            @pl.loop(0, 4)
            def _(j):
                cols = pl.ds(al(j * 256, 256), 256)
                at, part = grad_part(k, n, cols)
                gacc[at, cols] = part if first else gacc[at, cols] + part

    def gf(j):
        need_d(3)
        cols = pl.ds(256 * j, 256)

        @pl.loop(0, 3)
        def _(n):
            at, part = grad_part(3, n, cols)
            gs[j, at, :] = (gacc[at, cols] + part).astype(BF16)

        here = pl.ds(al(x * 768, 256), 768)
        for q, out in enumerate((g_gate, g_up)):
            src = gs.at[j, :, pl.ds(128 * q, 128)]
            if j:
                send(("gw", j, q), src, out.at[here, :], dev(dx=j))
            else:
                move(src, out.at[here, :])

    def gd():
        for k in range(4):
            recv(("ch", k), hid.at[half(k, 1 - c), :])

        @pl.loop(0, 4)
        def _(m):
            there = (y + m) % 4
            g_down[pl.ds(al(there * 256, 256), 256), :] = lax.dot_general(
                hid[:, pl.ds(al(m * 256, 256), 256)], og[...].reshape(2048, 384), (((0,), (0,)), ((), ())),
                preferred_element_type=F32,
            ).astype(BF16)

    steps = (
        (st_w, 1), (sty, 0), (st_w, 0), (st_og,), (stz, 1), (fw, 1), (sty, 3), (stz, 2), (sty, 1), (stz, 3),
        (stz, 0), (sty, 2), (fw, 0), (ox, 0), (fi, 1), (fz, 1), (fi, 0), (fw, 3), (ox, 1), (fw, 2), (b1, 0),
        (fz, 0), (ox, 2), (g1, 0), (fi, 2), (b2, 0), (g2, 0), (b1, 1), (fz, 2), (b1, 2), (g1, 1), (b2, 1),
        (ox, 3), (g3, 0), (g2, 1), (b3, 0), (g1, 2), (fi, 3), (b2, 2), (b3, 1), (b1, 3), (g2, 2), (fz, 3),
        (e, 0), (g1, 3), (b2, 3), (g3, 1), (a2y, 0), (a2x, 0), (g3, 2), (e, 1), (b3, 2), (g2, 3), (a2x, 1),
        (b3, 3), (a2y, 1), (e, 2), (afy, 0), (g3, 3), (afx, 0), (a3, 0), (a2y, 2), (a2x, 2), (afx, 1), (e, 3),
        (afy, 1), (gp, 0), (afx, 2), (a3, 1), (afy, 2), (a4, 1), (a2y, 3), (a2x, 3), (xk, 1), (xk, 0), (a3, 2),
        (afx, 3), (gp, 1), (a3, 3), (gp, 2), (afy, 3), (gf, 3), (xk, 3), (gf, 2), (xk, 2), (a4, 0), (a4, 3),
        (a4, 2), (gd,), (gf, 1), (x2, 0), (x2, 3), (x2, 2), (x2, 1), (xt, 1), (xt, 3), (gf, 0), (xt, 0), (xt, 2),
    )
    for step in steps:
        step[0](*step[1:])

    for j in (1, 3, 2):
        for q, out in enumerate((g_gate, g_up)):
            recv(("gw", j, q), out.at[pl.ds(al(((x - j + 4) % 4) * 768, 256), 768), :])
    for copy in local[n_first:]:
        copy.wait()
    done = [id(copy) for copy in uses[:-N_SLOT]]
    for copy in sent:
        if id(copy) not in done:
            copy.wait_send()
    assert len(index) <= N_SEM, len(index)


def shards(inputs, out_grad, w_gate, w_up, w_down):
    v = pltpu.VMEM
    any_ = pl.BlockSpec(memory_space=pl.ANY)
    vm = pl.BlockSpec(memory_space=pltpu.VMEM)
    return pl.pallas_call(
        kernel,
        name="swiglu_back",
        out_shape=(
            jax.ShapeDtypeStruct((256, 768), BF16),
            jax.ShapeDtypeStruct((3072, 128), BF16),
            jax.ShapeDtypeStruct((3072, 128), BF16),
            jax.ShapeDtypeStruct((1024, 384), BF16),
        ),
        in_specs=[any_] * 5,
        out_specs=(vm, any_, any_, vm),
        scratch_shapes=[
            v((2048, 768), BF16),
            v((768, 1024), BF16),
            v((4, 8, 64, 384), BF16),
            v((1024, 384), BF16),
            v((N_SLOT, 512, 1024), F32),
            v((8, 256, 1024), F32),
            v((8, 256, 1024), BF16),
            v((4, 3, 256, 256), BF16),
            v((4, 3, 256, 256), BF16),
            v((4, 256, 256), F32),
            v((4, 128, 256), F32),
            v((4, 256, 256), F32),
            v((4, 3, 128, 128), F32),
            v((2048, 1024), BF16),
            v((2048, 1024), BF16),
            v((4, 256, 768), BF16),
            v((4, 256, 768), BF16),
            v((max(1, len(DZ)), 256, 768), F32),
            v((max(1, len(DY)), 2, 4, 64, 768), F32),
            v((4, 2, 4, 64, 768), BF16),
            v((4, 3, 2, 64, 768), BF16),
            v((4, 768, 256), BF16),
            v((768, 1024), F32),
            pltpu.SemaphoreType.DMA((N_SEM,)),
            pltpu.SemaphoreType.DMA((N_SEM,)),
            pltpu.SemaphoreType.DMA((16,)),
        ],
        compiler_params=pltpu.CompilerParams(collective_id=0, has_side_effects=True, vmem_limit_bytes=61 * 2**20),
        cost_estimate=pl.CostEstimate(flops=13 * 10**9, bytes_accessed=8 * 2**20, transcendentals=65536),
    )(inputs, out_grad.reshape(4, 4, 16, 3072), w_gate, w_up, w_down)


def solution(mesh):
    in_specs = (
        P("tok", "in"),
        P("tok", "in"),
        P("in", ("out", "tok")),
        P("in", ("out", "tok")),
        P("out", ("in", "tok")),
    )
    out_specs = (
        P("tok", ("in", "out")),
        P("in", ("out", "tok")),
        P("in", ("out", "tok")),
        P("out", ("in", "tok")),
    )
    return jax.shard_map(shards, mesh=mesh, in_specs=in_specs, out_specs=out_specs, check_vma=False)
```

```python
import jax
import jax.numpy as jnp
from jax import lax
from jax.experimental import pallas as pl
from jax.experimental.pallas import tpu as pltpu
from jax.sharding import PartitionSpec as P

MESH = pl.DeviceIdType.MESH
F32 = jnp.float32
BF16 = jnp.bfloat16
N_SEM = 230
N_SLOT = 3
DZ = (0, 2)
DY = tuple(k for k in range(4) if k not in DZ)
Z_FIRST = (0, 1, 2, 3)
FWD_IN, FWD_XG, FWD_YG, FWD_OG = True, False, True, False


def kernel(
    inputs, out_grad, w_gate, w_up, w_down,
    d_in, g_gate, g_up, g_down,
    xin, wcat, og, wdn, pbuf, pr, s2, xr, yr, zg, zgr, zb, zbr, dcat, hid, dzs, dzr, dxo, dxf, dxs, dxr, gs, gacc,
    ssem, rsem, lsem,
):
    i = lax.axis_index("in")
    x = lax.axis_index("out")
    t = lax.axis_index("tok")
    h, c, y, l = i // 2, i % 2, t // 2, t % 2
    z = 2 * h + l

    def dev(dx=0, dy=0, dz=0, dc=0):
        zz = (z + dz) % 4
        return (2 * (zz // 2) + (c + dc) % 2, (x + dx) % 4, 2 * ((y + dy) % 4) + zz % 2)

    def lpart():
        return (i, x, 2 * y + 1 - l)

    def al(v, n):
        return pl.multiple_of(v, n)

    index, sent, local, got = {}, [], [], set()

    def sem_of(key):
        if key not in index:
            index[key] = len(index)
        return index[key]

    def send(key, src, dst, device):
        n = sem_of(key)
        copy = pltpu.make_async_remote_copy(
            src_ref=src, dst_ref=dst, send_sem=ssem.at[n], recv_sem=rsem.at[n],
            device_id=device, device_id_type=MESH,
        )
        copy.start()
        sent.append(copy)
        return copy

    def recv(key, dst):
        if key in got:
            return
        got.add(key)
        n = sem_of(key)
        pltpu.make_async_remote_copy(
            src_ref=dst, dst_ref=dst, send_sem=ssem.at[n], recv_sem=rsem.at[n],
            device_id=dev(dc=1), device_id_type=MESH,
        ).wait_recv()

    def move(src, dst):
        copy = pltpu.make_async_copy(src, dst, lsem.at[len(local)])
        copy.start()
        local.append(copy)
        return copy

    def rows(s, yy, ll):
        return pl.ds(al(s * 512 + ll * 256 + yy * 64, 64), 64)

    def half(s, part):
        return pl.ds(al(s * 512 + part * 256, 256), 256)

    cols_in = pl.ds(al(x * 768, 128), 768)
    mine16 = pl.ds(al(x * 16, 16), 16)
    own_in = []
    for s in range(4):
        here = pl.ds(64 * s, 64)
        own_in.append(move(inputs.at[here, cols_in], xin.at[rows(s, y, l), :]))
    own_og = move(out_grad.at[:, x, :, pl.ds(al(t * 384, 128), 384)], og.at[:, 4 * l + y, mine16, :])
    own_dn = move(w_down, wdn)
    own_w = [
        move(w.at[pl.ds(al(x * 768, 256), 768), :], wcat.at[:, pl.ds(128 * q, 128)])
        for q, w in enumerate((w_gate, w_up))
    ]
    n_first = len(local)

    barrier = pltpu.get_barrier_semaphore()
    peers = [dev(dc=1)]
    peers += [dev(dx=m) for m in (1, 2, 3)]
    peers += [dev(dy=m) for m in (1, 2, 3)]
    peers += [dev(dz=m) for m in (1, 2, 3)]
    cross = [(i, x, 2 * ((y + m) % 4) + 1 - l) for m in (1, 2, 3)]
    peers += cross
    for peer in peers:
        pl.semaphore_signal(barrier, inc=1, device_id=peer, device_id_type=MESH)
    pl.semaphore_wait(barrier, len(peers))

    def og_cols(yy, ll):
        return pl.ds(al((2 * yy + ll) * 384, 128), 384)

    def st_og():
        send(("og", 0, 1), out_grad.at[:, x, :, og_cols(y, 1 - l)], og.at[:, 4 * l + y, mine16, :], lpart())
        for m in (2, 1, 3):
            there = (y + m) % 4
            send(("og", m, 0), out_grad.at[:, x, :, og_cols(there, l)], og.at[:, 4 * l + y, mine16, :], dev(dy=m))
            send(("og", m, 1), out_grad.at[:, x, :, og_cols(there, 1 - l)], og.at[:, 4 * l + y, mine16, :], cross[m - 1])

    def take_og():
        own_og.wait()
        recv(("og", 0, 1), og.at[:, 4 * (1 - l) + y, mine16, :])
        for m in (1, 3, 2):
            yy = (y - m + 4) % 4
            recv(("og", m, 0), og.at[:, 4 * l + yy, mine16, :])
            recv(("og", m, 1), og.at[:, 4 * (1 - l) + yy, mine16, :])

    def og_part(s, j, lo=0, n=16):
        return og.at[s, :, pl.ds(al(((x + j) % 4) * 16 + lo, n), n), :]

    def ox(s):
        if s == 0:
            take_og()
        for j in (1, 3) if FWD_OG else (2, 1, 3):
            send(("ox", s, j), og_part(s, 0), og_part(s, 0), dev(dx=j))

    def fo(s):
        if FWD_OG:
            for j in (1, 3):
                part = og.at[s, pl.ds(0 if j == 1 else 4, 4), pl.ds(al(((x - j + 4) % 4) * 16, 16), 16), :]
                recv(("ox", s, j), og_part(s, 4 - j))
                send(("of", s, j), part, part, dev(dx=j))

    def wait_og(s):
        if FWD_OG:
            for j in (1, 3):
                recv(("of", s, j), og.at[s, pl.ds(0 if j == 1 else 4, 4), pl.ds(al(((x + 2) % 4) * 16, 16), 16), :])
        else:
            for j in (1, 3, 2):
                recv(("ox", s, j), og_part(s, 4 - j))

    def stz(s):
        here = pl.ds(64 * s, 64)
        at = rows(s, y, l)
        send(("in", s, 0, 1), inputs.at[here, cols_in], xin.at[at, :], lpart())

    def sty(s):
        here = pl.ds(64 * s, 64)
        at = rows(s, y, l)
        for m in (1, 3) if FWD_IN else (2, 1, 3):
            send(("in", s, m, 0), inputs.at[here, cols_in], xin.at[at, :], dev(dy=m))

    def st_w(q):
        w = (w_gate, w_up)[q]
        for j in (2, 1, 3):
            send(
                ("w", j, q), w.at[pl.ds(al(((x + j) % 4) * 768, 256), 768), :],
                wcat.at[:, pl.ds(256 * (4 - j) + 128 * q, 128)], dev(dx=j),
            )

    def part_rows(s, yy, ll, m):
        return pl.ds(al(s * 512 + ll * 256 + yy * 64 + (0 if m == 1 else 32), 32), 32)

    def fw(s):
        if s in Z_FIRST:
            at = rows(s, y, 1 - l)
            recv(("in", s, 0, 1), xin.at[at, :])
            for m in (1, 3) if FWD_IN else (2, 1, 3):
                send(("in", s, m, 1), xin.at[at, :], xin.at[at, :], dev(dy=m))

    def fi(s):
        if FWD_IN:
            for q in (0, 1) if s in Z_FIRST else (0,):
                for m in (1, 3):
                    yy, ll = (y - m + 4) % 4, (1 - l if q else l)
                    recv(("in", s, m, q), xin.at[rows(s, yy, ll), :])
                    at = part_rows(s, yy, ll, m)
                    send(("if", s, m, q), xin.at[at, :], xin.at[at, :], dev(dy=m))

    def far_in(s, q):
        yy, ll = (y + 2) % 4, (1 - l if q else l)
        if FWD_IN:
            for m in (1, 3):
                recv(("if", s, m, q), xin.at[part_rows(s, yy, ll, m), :])
        else:
            recv(("in", s, 2, q), xin.at[rows(s, yy, ll), :])

    def fz(s):
        if s not in Z_FIRST:
            for m in (1, 3, 2):
                at = rows(s, (y - m + 4) % 4, l)
                if m == 2:
                    far_in(s, 0)
                elif not FWD_IN:
                    recv(("in", s, m, 0), xin.at[at, :])
                send(("in", s, m, 1), xin.at[at, :], xin.at[at, :], lpart())

    def wait_in(s):
        own_in[s].wait()
        if s in Z_FIRST:
            if not FWD_IN:
                for m in (1, 3):
                    for q in (0, 1):
                        recv(("in", s, m, q), xin.at[rows(s, (y - m + 4) % 4, 1 - l if q else l), :])
            far_in(s, 0)
            far_in(s, 1)
        else:
            recv(("in", s, 0, 1), xin.at[rows(s, y, 1 - l), :])
            for m in (1, 3, 2):
                recv(("in", s, m, 1), xin.at[rows(s, (y - m + 4) % 4, 1 - l), :])

    uses = []

    def partial_slot():
        n = len(uses)
        if n >= N_SLOT:
            uses[n - N_SLOT].wait_send()
        return n % N_SLOT

    def core_send(slot, n):
        uses.append(send(("cr", n), pbuf.at[slot, pl.ds(al((1 - c) * 256, 256), 256), :], pr.at[n], dev(dc=1)))

    slots, seen = {}, []

    def b1(s):
        wait_og(s)
        if s == 0:
            own_dn.wait()
        slot = partial_slot()
        slots["b", s] = slot

        @pl.loop(0, 4)
        def _(m):
            there = (y + m) % 4
            pbuf[slot, :, pl.ds(al(m * 256, 256), 256)] = lax.dot_general(
                og[s].reshape(512, 384), wdn[pl.ds(al(there * 256, 256), 256), :],
                (((1,), (1,)), ((), ())), preferred_element_type=F32,
            )

        core_send(slot, 4 + s)

    def g1(s):
        wait_in(s)
        if s == 0:
            for copy in own_w:
                copy.wait()
            for j in (1, 3, 2):
                for q in (0, 1):
                    recv(("w", j, q), wcat.at[:, pl.ds(256 * (4 - j) + 128 * q, 128)])
        slot = partial_slot()
        slots["g", s] = slot

        @pl.loop(0, 4)
        def _(n):
            at = pl.ds(al(n * 256, 256), 256)
            pbuf[slot, :, at] = jnp.dot(xin[pl.ds(512 * s, 512), :], wcat[:, at], preferred_element_type=F32)

        core_send(slot, s)

    def core_sum(slot, n):
        recv(("cr", n), pr.at[n])

        @pl.loop(0, 8)
        def _(r):
            at = pl.ds(al(r * 32, 32), 32)
            mine = pl.ds(al(c * 256 + r * 32, 32), 32)
            total = pbuf[slot, mine, :] + pr[n, at, :]
            pr[n, at, :] = total
            s2[n, at, :] = total.astype(BF16)

    def b2(s):
        core_sum(slots["b", s], 4 + s)
        for m in (2, 1, 3):
            send(("yr", s, m), s2.at[4 + s, :, pl.ds(256 * m, 256)], yr.at[s, m - 1], dev(dy=m))

    def g2(s):
        core_sum(slots["g", s], s)
        for j in (2, 1, 3):
            send(("xr", s, j), s2.at[s, :, pl.ds(256 * j, 256)], xr.at[s, j - 1], dev(dx=j))

    def b3(k):
        for m in (1, 3, 2):
            recv(("yr", k, m), yr.at[k, m - 1])
        zb[k] = (pr[4 + k, :, 0:256] + yr[k, 0].astype(F32)) + (yr[k, 1].astype(F32) + yr[k, 2].astype(F32))
        for d in (2, 1, 3):
            zz = (z + d) % 4
            send(
                ("zb", k, d), zb.at[k, pl.ds(al((zz // 2) * 128, 128), 128), pl.ds(al((zz % 2) * 128, 128), 128)],
                zbr.at[k, d - 1], dev(dz=d),
            )

    def g3(k):
        for j in (1, 3, 2):
            recv(("xr", k, j), xr.at[k, j - 1])
        zg[k] = (pr[k, :, 0:256] + xr[k, 0].astype(F32)) + (xr[k, 1].astype(F32) + xr[k, 2].astype(F32))
        send(("zg", k), zg.at[k, pl.ds(al((1 - h) * 128, 128), 128), :], zgr.at[k], dev(dz=2))

    def e(k):
        recv(("zg", k), zgr.at[k])
        for d in (1, 2, 3):
            recv(("zb", k, d), zbr.at[k, d - 1])
        mine = pl.ds(al(h * 128, 128), 128)
        both = zg[k, mine, :] + zgr[k]
        gate, up = both[:, :128], both[:, 128:]
        back = (zb[k, mine, pl.ds(al(l * 128, 128), 128)] + zbr[k, 0]) + (zbr[k, 1] + zbr[k, 2])
        sig = jax.nn.sigmoid(gate)
        act = gate * sig
        at = pl.ds(al(k * 512 + c * 256 + h * 128, 128), 128)
        dcat[at, 0:128] = (back * up * sig * (1.0 + gate * (1.0 - sig))).astype(BF16)
        dcat[at, 128:256] = (back * act).astype(BF16)
        cols = pl.ds(al(l * 128, 128), 128)
        hid[at, cols] = (act * up).astype(BF16)
        send(("ag", k), dcat.at[at, 0:256], dcat.at[at, 0:256], dev(dz=2))
        for d in (2, 1, 3):
            send(("ah", k, d), hid.at[at, cols], hid.at[at, cols], dev(dz=d))

    def a2x(k):
        there = pl.ds(al(k * 512 + c * 256 + (1 - h) * 128, 128), 128)
        recv(("ag", k), dcat.at[there, 0:256])
        for j in (1, 3) if FWD_XG else (2, 1, 3):
            send(("xg", k, j), dcat.at[half(k, c), 0:256], dcat.at[half(k, c), pl.ds(256 * (4 - j), 256)], dev(dx=j))

    def a2y(k):
        for d in (1, 2, 3):
            zz = (z - d + 4) % 4
            at = pl.ds(al(k * 512 + c * 256 + (zz // 2) * 128, 128), 128)
            recv(("ah", k, d), hid.at[at, pl.ds(al((zz % 2) * 128, 128), 128)])
        for m in (1, 3) if FWD_YG else (2, 1, 3):
            send(("yg", k, m), hid.at[half(k, c), 0:256], hid.at[half(k, c), pl.ds(256 * (4 - m), 256)], dev(dy=m))

    def fwd_half(k, j):
        return pl.ds(al(k * 512 + c * 256 + (0 if j == 1 else 128), 128), 128)

    def af(k, on, name, buf, to):
        if on:
            for j in (1, 3):
                recv((name, k, j), buf.at[half(k, c), pl.ds(256 * (4 - j), 256)])
                send((name + "f", k, j), buf.at[fwd_half(k, j), pl.ds(256 * (4 - j), 256)], buf.at[fwd_half(k, j), pl.ds(512, 256)], to(j))

    def afx(k):
        af(k, FWD_XG, "xg", dcat, lambda j: dev(dx=j))

    def afy(k):
        af(k, FWD_YG, "yg", hid, lambda j: dev(dy=j))

    def gathered(k, on, name, buf):
        if on:
            for j in (1, 3):
                recv((name + "f", k, j), buf.at[fwd_half(k, j), pl.ds(512, 256)])
        else:
            for j in (1, 3, 2):
                recv((name, k, j), buf.at[half(k, c), pl.ds(256 * (4 - j), 256)])

    def a3(k):
        gathered(k, FWD_XG, "xg", dcat)
        send(("cg", k), dcat.at[half(k, c), :], dcat.at[half(k, c), :], dev(dc=1))

    def a4(k):
        gathered(k, FWD_YG, "yg", hid)
        send(("ch", k), hid.at[half(k, c), :], hid.at[half(k, c), :], dev(dc=1))

    def need_d(k):
        recv(("cg", k), dcat.at[half(k, 1 - c), :])

    def times_w(lhs, n):
        return lax.dot_general(
            lhs, wcat[pl.ds(al(n * 256, 256), 256), :], (((1,), (1,)), ((), ())), preferred_element_type=F32
        )

    def xk(k):
        need_d(k)
        if k in DZ:
            n_k = DZ.index(k)

            @pl.loop(0, 3)
            def _(n):
                at = pl.ds(al(n * 256, 256), 256)
                part = times_w(jnp.concatenate([dcat[half(k, 1 - l), :], dcat[half(k, l), :]], axis=0), n)
                dzs[k, :, at] = part[:256].astype(BF16)
                dxo[n_k, :, at] = part[256:]

            send(("dz", k), dzs.at[k], dzr.at[k], lpart())
        else:
            n_k = DY.index(k)

            @pl.loop(0, 3)
            def _(n):
                at = pl.ds(al(n * 256, 256), 256)
                part = times_w(dcat[pl.ds(512 * k, 512), :], n).reshape(2, 4, 64, 256)
                dxs[k, :, :, :, at] = part.astype(BF16)
                dxf[n_k, :, :, :, at] = part

            for m in (2, 1, 3):
                send(("dx", k, m), dxs.at[k, :, (y + m) % 4], dxr.at[k, m - 1], dev(dy=m))

    def x2(k):
        if k in DZ:
            n_k = DZ.index(k)
            recv(("dz", k), dzr.at[k])

            @pl.loop(0, 4)
            def _(r):
                at = pl.ds(al(r * 64, 64), 64)
                total = dxo[n_k, at, :] + dzr[k, at, :].astype(F32)
                dxo[n_k, at, :] = total
                dxs[k, 0, r] = total.astype(BF16)

            for m in (2, 1, 3):
                send(("dx", k, m), dxs.at[k, 0, (y + m) % 4], dxr.at[k, m - 1, 0], dev(dy=m))
        else:
            n_k = DY.index(k)
            for m in (1, 3, 2):
                recv(("dx", k, m), dxr.at[k, m - 1])
            total = (dxf[n_k, :, y] + dxr[k, 0].astype(F32)) + (dxr[k, 1].astype(F32) + dxr[k, 2].astype(F32))
            dxf[n_k, :, 0] = total
            dxs[k, :, y] = total.astype(BF16)
            send(("dz", k), dxs.at[k, 1 - l, y], dzr.at[k, 0:64], lpart())

    def xt(k):
        at = pl.ds(64 * k, 64)
        if k in DZ:
            for m in (1, 3, 2):
                recv(("dx", k, m), dxr.at[k, m - 1, 0])
            d_in[at, :] = (
                (dxo[DZ.index(k), pl.ds(al(y * 64, 64), 64), :] + dxr[k, 0, 0].astype(F32))
                + (dxr[k, 1, 0].astype(F32) + dxr[k, 2, 0].astype(F32))
            ).astype(BF16)
        else:
            recv(("dz", k), dzr.at[k, 0:64])
            d_in[at, :] = (dxf[DY.index(k), l, 0] + dzr[k, 0:64].astype(F32)).astype(BF16)

    def grad_part(k, n, cols):
        at = pl.ds(al(n * 256, 256), 256)
        return at, lax.dot_general(
            xin[pl.ds(512 * k, 512), at], dcat[pl.ds(512 * k, 512), cols], (((0,), (0,)), ((), ())),
            preferred_element_type=F32,
        )

    begun = []

    def gp(k):
        need_d(k)
        first = not begun
        begun.append(k)

        @pl.loop(0, 3)
        def _(n):
            @pl.loop(0, 4)
            def _(j):
                cols = pl.ds(al(j * 256, 256), 256)
                at, part = grad_part(k, n, cols)
                gacc[at, cols] = part if first else gacc[at, cols] + part

    def gf(j):
        need_d(3)
        cols = pl.ds(256 * j, 256)

        @pl.loop(0, 3)
        def _(n):
            at, part = grad_part(3, n, cols)
            gs[j, at, :] = (gacc[at, cols] + part).astype(BF16)

        here = pl.ds(al(x * 768, 256), 768)
        for q, out in enumerate((g_gate, g_up)):
            src = gs.at[j, :, pl.ds(128 * q, 128)]
            if j:
                send(("gw", j, q), src, out.at[here, :], dev(dx=j))
            else:
                move(src, out.at[here, :])

    def gd():
        for k in range(4):
            recv(("ch", k), hid.at[half(k, 1 - c), :])

        @pl.loop(0, 4)
        def _(m):
            there = (y + m) % 4
            g_down[pl.ds(al(there * 256, 256), 256), :] = lax.dot_general(
                hid[:, pl.ds(al(m * 256, 256), 256)], og[...].reshape(2048, 384), (((0,), (0,)), ((), ())),
                preferred_element_type=F32,
            ).astype(BF16)

    steps = (
        (st_w, 1), (sty, 0), (st_w, 0), (st_og,), (stz, 1), (fw, 1), (sty, 3), (stz, 2), (sty, 1), (stz, 3),
        (stz, 0), (sty, 2), (fw, 0), (ox, 0), (fi, 1), (fz, 1), (fi, 0), (fw, 3), (ox, 1), (fw, 2), (b1, 0),
        (fz, 0), (ox, 2), (g1, 0), (fi, 2), (b2, 0), (g2, 0), (b1, 1), (fz, 2), (b1, 2), (g1, 1), (b2, 1),
        (ox, 3), (g3, 0), (g2, 1), (b3, 0), (g1, 2), (fi, 3), (b2, 2), (b3, 1), (b1, 3), (g2, 2), (fz, 3),
        (e, 0), (g1, 3), (b2, 3), (g3, 1), (a2y, 0), (a2x, 0), (g3, 2), (e, 1), (b3, 2), (g2, 3), (a2x, 1),
        (b3, 3), (a2y, 1), (e, 2), (afy, 0), (g3, 3), (afx, 0), (a3, 0), (a2y, 2), (a2x, 2), (afx, 1), (e, 3),
        (afy, 1), (gp, 0), (afx, 2), (a3, 1), (afy, 2), (a4, 1), (a2y, 3), (a2x, 3), (xk, 1), (xk, 0), (a3, 2),
        (afx, 3), (gp, 1), (a3, 3), (gp, 2), (afy, 3), (gf, 3), (xk, 3), (gf, 2), (xk, 2), (a4, 0), (a4, 3),
        (a4, 2), (gd,), (gf, 1), (x2, 0), (x2, 3), (x2, 2), (x2, 1), (xt, 1), (xt, 3), (gf, 0), (xt, 0), (xt, 2),
    )
    for step in steps:
        step[0](*step[1:])

    for j in (1, 3, 2):
        for q, out in enumerate((g_gate, g_up)):
            recv(("gw", j, q), out.at[pl.ds(al(((x - j + 4) % 4) * 768, 256), 768), :])
    for copy in local[n_first:]:
        copy.wait()
    done = [id(copy) for copy in uses[:-N_SLOT]]
    for copy in sent:
        if id(copy) not in done:
            copy.wait_send()
    assert len(index) <= N_SEM, len(index)


def finish(*refs):
    ins, outs = [], []
    for k, (src, dst) in enumerate(zip(refs[:4], refs[4:8])):
        buf, n = refs[8 + k], src.shape[0] // 4
        for part in range(4):
            at = pl.ds(part * n, n)
            ins.append(pltpu.make_async_copy(src.at[at], buf.at[at], refs[12].at[len(ins)]))
            outs.append(pltpu.make_async_copy(buf.at[at], dst.at[at], refs[13].at[len(outs)]))
            ins[-1].start()
    for first, then in zip(ins, outs):
        first.wait()
        then.start()
    for then in outs:
        then.wait()


def shards(inputs, out_grad, w_gate, w_up, w_down):
    v = pltpu.VMEM
    any_ = pl.BlockSpec(memory_space=pl.ANY)
    vm = pl.BlockSpec(memory_space=pltpu.VMEM)
    outs = pl.pallas_call(
        kernel,
        name="swiglu_back",
        out_shape=(
            jax.ShapeDtypeStruct((256, 768), BF16),
            jax.ShapeDtypeStruct((3072, 128), BF16),
            jax.ShapeDtypeStruct((3072, 128), BF16),
            jax.ShapeDtypeStruct((1024, 384), BF16),
        ),
        in_specs=[any_] * 5,
        out_specs=(vm, any_, any_, vm),
        scratch_shapes=[
            v((2048, 768), BF16),
            v((768, 1024), BF16),
            v((4, 8, 64, 384), BF16),
            v((1024, 384), BF16),
            v((N_SLOT, 512, 1024), F32),
            v((8, 256, 1024), F32),
            v((8, 256, 1024), BF16),
            v((4, 3, 256, 256), BF16),
            v((4, 3, 256, 256), BF16),
            v((4, 256, 256), F32),
            v((4, 128, 256), F32),
            v((4, 256, 256), F32),
            v((4, 3, 128, 128), F32),
            v((2048, 1024), BF16),
            v((2048, 1024), BF16),
            v((4, 256, 768), BF16),
            v((4, 256, 768), BF16),
            v((max(1, len(DZ)), 256, 768), F32),
            v((max(1, len(DY)), 2, 4, 64, 768), F32),
            v((4, 2, 4, 64, 768), BF16),
            v((4, 3, 2, 64, 768), BF16),
            v((4, 768, 256), BF16),
            v((768, 1024), F32),
            pltpu.SemaphoreType.DMA((N_SEM,)),
            pltpu.SemaphoreType.DMA((N_SEM,)),
            pltpu.SemaphoreType.DMA((16,)),
        ],
        compiler_params=pltpu.CompilerParams(collective_id=0, has_side_effects=True, vmem_limit_bytes=61 * 2**20),
        cost_estimate=pl.CostEstimate(flops=13 * 10**9, bytes_accessed=8 * 2**20, transcendentals=65536),
    )(inputs, out_grad.reshape(4, 4, 16, 3072), w_gate, w_up, w_down)
    return pl.pallas_call(
        finish,
        name="results",
        out_shape=tuple(jax.ShapeDtypeStruct(v.shape, v.dtype) for v in outs),
        in_specs=[any_] * 4,
        out_specs=(any_,) * 4,
        scratch_shapes=[v(o.shape, o.dtype) for o in outs] + [pltpu.SemaphoreType.DMA((16,))] * 2,
        cost_estimate=pl.CostEstimate(flops=0, bytes_accessed=5 * 2**20, transcendentals=0),
    )(*outs)


def solution(mesh):
    in_specs = (
        P("tok", "in"),
        P("tok", "in"),
        P("in", ("out", "tok")),
        P("in", ("out", "tok")),
        P("out", ("in", "tok")),
    )
    out_specs = (
        P("tok", ("in", "out")),
        P("in", ("out", "tok")),
        P("in", ("out", "tok")),
        P("out", ("in", "tok")),
    )
    return jax.shard_map(shards, mesh=mesh, in_specs=in_specs, out_specs=out_specs, check_vma=False)
```

```python
import jax
import jax.numpy as jnp
from jax import lax
from jax.experimental import pallas as pl
from jax.experimental.pallas import tpu as pltpu
from jax.sharding import PartitionSpec as P

MESH = pl.DeviceIdType.MESH
F32 = jnp.float32
BF16 = jnp.bfloat16
N_SEM = 230
N_SLOT = 3
OX = (2, 4)
DZ = (0, 2, 3)
DY = tuple(k for k in range(4) if k not in DZ)
Z_FIRST = (0, 1, 2, 3)
FWD_IN, FWD_XG, FWD_YG, FWD_OG = True, False, True, False


def kernel(
    inputs, out_grad, w_gate, w_up, w_down,
    d_in, g_gate, g_up, g_down,
    xin, wcat, og, wdn, pbuf, pr, s2, xr, yr, zg, zgr, zb, zbr, yb, dcat, hid, dzs, dzr, dxo, dxf, dxs, dxr, gs, gacc,
    ssem, rsem, lsem,
):
    i = lax.axis_index("in")
    x = lax.axis_index("out")
    t = lax.axis_index("tok")
    h, c, y, l = i // 2, i % 2, t // 2, t % 2
    z = 2 * h + l

    def dev(dx=0, dy=0, dz=0, dc=0):
        zz = (z + dz) % 4
        return (2 * (zz // 2) + (c + dc) % 2, (x + dx) % 4, 2 * ((y + dy) % 4) + zz % 2)

    def lpart():
        return (i, x, 2 * y + 1 - l)

    def al(v, n):
        return pl.multiple_of(v, n)

    index, sent, local, got = {}, [], [], set()

    def sem_of(key):
        if key not in index:
            index[key] = len(index)
        return index[key]

    def send(key, src, dst, device):
        n = sem_of(key)
        copy = pltpu.make_async_remote_copy(
            src_ref=src, dst_ref=dst, send_sem=ssem.at[n], recv_sem=rsem.at[n],
            device_id=device, device_id_type=MESH,
        )
        copy.start()
        sent.append(copy)
        return copy

    def recv(key, dst):
        if key in got:
            return
        got.add(key)
        n = sem_of(key)
        pltpu.make_async_remote_copy(
            src_ref=dst, dst_ref=dst, send_sem=ssem.at[n], recv_sem=rsem.at[n],
            device_id=dev(dc=1), device_id_type=MESH,
        ).wait_recv()

    def move(src, dst):
        copy = pltpu.make_async_copy(src, dst, lsem.at[len(local)])
        copy.start()
        local.append(copy)
        return copy

    def rows(s, yy, ll):
        return pl.ds(al(s * 512 + ll * 256 + yy * 64, 64), 64)

    def half(s, part):
        return pl.ds(al(s * 512 + part * 256, 256), 256)

    cols_in = pl.ds(al(x * 768, 128), 768)
    by_x = pl.ds(OX[0], OX[1] - OX[0])
    own_in = []
    for s in range(4):
        here = pl.ds(64 * s, 64)
        own_in.append(move(inputs.at[here, cols_in], xin.at[rows(s, y, l), :]))
    own_og = {}
    for s in range(4):
        if not OX[0] <= s < OX[1]:
            own_og[s] = move(out_grad.at[s, :, :, pl.ds(al(t * 384, 128), 384)], og.at[s, 4 * l + y])
    if OX[0] < OX[1]:
        own_og[-1] = move(out_grad.at[by_x, x, :, pl.ds(al(t * 384, 128), 384)], og.at[by_x, 4 * l + y, x])
    own_dn = move(w_down, wdn)
    own_w = [
        move(w.at[pl.ds(al(x * 768, 256), 768), :], wcat.at[:, pl.ds(128 * q, 128)])
        for q, w in enumerate((w_gate, w_up))
    ]
    n_first = len(local)

    barrier = pltpu.get_barrier_semaphore()
    peers = [dev(dc=1)]
    peers += [dev(dx=m) for m in (1, 2, 3)]
    peers += [dev(dy=m) for m in (1, 2, 3)]
    peers += [dev(dz=m) for m in (1, 2, 3)]
    cross = [(i, x, 2 * ((y + m) % 4) + 1 - l) for m in (1, 2, 3)]
    peers += cross
    for peer in peers:
        pl.semaphore_signal(barrier, inc=1, device_id=peer, device_id_type=MESH)
    pl.semaphore_wait(barrier, len(peers))

    def og_cols(yy, ll):
        return pl.ds(al((2 * yy + ll) * 384, 128), 384)

    def og_from(s, yy, ll):
        return og.at[s, 4 * ll + yy] if s >= 0 else og.at[by_x, 4 * ll + yy, x]

    def og_src(s, yy, ll):
        return out_grad.at[s, :, :, og_cols(yy, ll)] if s >= 0 else out_grad.at[by_x, x, :, og_cols(yy, ll)]

    def st_og(s):
        send(("og", s, 0, 1), og_src(s, y, 1 - l), og_from(s, y, l), lpart())
        for m in (2, 1, 3):
            there = (y + m) % 4
            send(("og", s, m, 0), og_src(s, there, l), og_from(s, y, l), dev(dy=m))
            send(("og", s, m, 1), og_src(s, there, 1 - l), og_from(s, y, l), cross[m - 1])

    def take_og(s):
        if s not in taken:
            own_og[s].wait()
            taken.append(s)
        recv(("og", s, 0, 1), og_from(s, y, 1 - l))
        for m in (1, 3, 2):
            yy = (y - m + 4) % 4
            recv(("og", s, m, 0), og_from(s, yy, l))
            recv(("og", s, m, 1), og_from(s, yy, 1 - l))

    taken = []

    def og_part(s, j):
        return og.at[s, :, (x + j) % 4]

    def ox(s):
        if OX[0] <= s < OX[1]:
            take_og(-1)
            for j in (1, 3) if FWD_OG else (2, 1, 3):
                send(("ox", s, j), og_part(s, 0), og_part(s, 0), dev(dx=j))

    def og_far(s, j):
        return og.at[s, pl.ds(0 if j == 1 else 4, 4), (x - j + 4) % 4]

    def fo(s):
        if FWD_OG and OX[0] <= s < OX[1]:
            for j in (1, 3):
                recv(("ox", s, j), og_part(s, 4 - j))
                send(("of", s, j), og_far(s, j), og_far(s, j), dev(dx=j))

    def wait_og(s):
        if not OX[0] <= s < OX[1]:
            take_og(s)
        elif FWD_OG:
            for j in (1, 3):
                recv(("of", s, j), og.at[s, pl.ds(0 if j == 1 else 4, 4), (x + 2) % 4])
        else:
            for j in (1, 3, 2):
                recv(("ox", s, j), og_part(s, 4 - j))

    def stz(s):
        here = pl.ds(64 * s, 64)
        at = rows(s, y, l)
        send(("in", s, 0, 1), inputs.at[here, cols_in], xin.at[at, :], lpart())

    def sty(s):
        here = pl.ds(64 * s, 64)
        at = rows(s, y, l)
        for m in (1, 3) if FWD_IN else (2, 1, 3):
            send(("in", s, m, 0), inputs.at[here, cols_in], xin.at[at, :], dev(dy=m))

    def st_w(q):
        w = (w_gate, w_up)[q]
        for j in (2, 1, 3):
            send(
                ("w", j, q), w.at[pl.ds(al(((x + j) % 4) * 768, 256), 768), :],
                wcat.at[:, pl.ds(256 * (4 - j) + 128 * q, 128)], dev(dx=j),
            )

    def part_rows(s, yy, ll, m):
        return pl.ds(al(s * 512 + ll * 256 + yy * 64 + (0 if m == 1 else 32), 32), 32)

    def fw(s):
        if s in Z_FIRST:
            at = rows(s, y, 1 - l)
            recv(("in", s, 0, 1), xin.at[at, :])
            for m in (1, 3) if FWD_IN else (2, 1, 3):
                send(("in", s, m, 1), xin.at[at, :], xin.at[at, :], dev(dy=m))

    def fi(s):
        if FWD_IN:
            for q in (0, 1) if s in Z_FIRST else (0,):
                for m in (1, 3):
                    yy, ll = (y - m + 4) % 4, (1 - l if q else l)
                    recv(("in", s, m, q), xin.at[rows(s, yy, ll), :])
                    at = part_rows(s, yy, ll, m)
                    send(("if", s, m, q), xin.at[at, :], xin.at[at, :], dev(dy=m))

    def far_in(s, q):
        yy, ll = (y + 2) % 4, (1 - l if q else l)
        if FWD_IN:
            for m in (1, 3):
                recv(("if", s, m, q), xin.at[part_rows(s, yy, ll, m), :])
        else:
            recv(("in", s, 2, q), xin.at[rows(s, yy, ll), :])

    def fz(s):
        if s not in Z_FIRST:
            for m in (1, 3, 2):
                at = rows(s, (y - m + 4) % 4, l)
                if m == 2:
                    far_in(s, 0)
                elif not FWD_IN:
                    recv(("in", s, m, 0), xin.at[at, :])
                send(("in", s, m, 1), xin.at[at, :], xin.at[at, :], lpart())

    def wait_in(s):
        own_in[s].wait()
        if s in Z_FIRST:
            if not FWD_IN:
                for m in (1, 3):
                    for q in (0, 1):
                        recv(("in", s, m, q), xin.at[rows(s, (y - m + 4) % 4, 1 - l if q else l), :])
            far_in(s, 0)
            far_in(s, 1)
        else:
            recv(("in", s, 0, 1), xin.at[rows(s, y, 1 - l), :])
            for m in (1, 3, 2):
                recv(("in", s, m, 1), xin.at[rows(s, (y - m + 4) % 4, 1 - l), :])

    uses = []

    def partial_slot():
        n = len(uses)
        if n >= N_SLOT:
            uses[n - N_SLOT].wait_send()
        return n % N_SLOT

    def core_send(slot, n):
        uses.append(send(("cr", n), pbuf.at[slot, pl.ds(al((1 - c) * 256, 256), 256), :], pr.at[n], dev(dc=1)))

    slots, seen = {}, []

    def b1(s):
        wait_og(s)
        if "dn" not in taken:
            own_dn.wait()
            taken.append("dn")
        slot = partial_slot()
        slots["b", s] = slot

        @pl.loop(0, 4)
        def _(m):
            there = (y + m) % 4
            part = lax.dot_general(
                og[s].reshape(512, 384), wdn[pl.ds(al(there * 256, 256), 256), :],
                (((1,), (1,)), ((), ())), preferred_element_type=F32,
            )
            for ll in (0, 1):
                pbuf[slot, :, pl.ds(al(ll * 512 + m * 128, 128), 128)] = part[:, 128 * ll : 128 * ll + 128]

        core_send(slot, 4 + s)

    def g1(s):
        wait_in(s)
        if "w" not in taken:
            taken.append("w")
            for copy in own_w:
                copy.wait()
            for j in (1, 3, 2):
                for q in (0, 1):
                    recv(("w", j, q), wcat.at[:, pl.ds(256 * (4 - j) + 128 * q, 128)])
        slot = partial_slot()
        slots["g", s] = slot

        @pl.loop(0, 4)
        def _(n):
            at = pl.ds(al(n * 256, 256), 256)
            pbuf[slot, :, at] = jnp.dot(xin[pl.ds(512 * s, 512), :], wcat[:, at], preferred_element_type=F32)

        core_send(slot, s)

    def core_sum(slot, n):
        recv(("cr", n), pr.at[n])

        @pl.loop(0, 8)
        def _(r):
            at = pl.ds(al(r * 32, 32), 32)
            mine = pl.ds(al(c * 256 + r * 32, 32), 32)
            total = pbuf[slot, mine, :] + pr[n, at, :]
            pr[n, at, :] = total
            s2[n, at, :] = total.astype(BF16)

    def b2(s):
        core_sum(slots["b", s], 4 + s)
        for d in (2, 1, 3):
            zz = (z + d) % 4
            at = (4 + s, pl.ds(al((zz // 2) * 128, 128), 128), pl.ds(al((zz % 2) * 512, 512), 512))
            send(("zb", s, d), s2.at[at], zbr.at[s, d - 1], dev(dz=d))

    def g2(s):
        core_sum(slots["g", s], s)
        for j in (2, 1, 3):
            send(("xr", s, j), s2.at[s, :, pl.ds(256 * j, 256)], xr.at[s, j - 1], dev(dx=j))

    def b3(k):
        for d in (1, 3, 2):
            recv(("zb", k, d), zbr.at[k, d - 1])
        mine = pr[4 + k, pl.ds(al(h * 128, 128), 128), pl.ds(al(l * 512, 512), 512)]
        total = (mine + zbr[k, 0].astype(F32)) + (zbr[k, 1].astype(F32) + zbr[k, 2].astype(F32))
        zb[k] = total[:, :128]
        yb[k] = total.astype(BF16)
        for m in (2, 1, 3):
            send(("yr", k, m), yb.at[k, :, pl.ds(128 * m, 128)], yr.at[k, m - 1], dev(dy=m))

    def g3(k):
        for j in (1, 3, 2):
            recv(("xr", k, j), xr.at[k, j - 1])
        zg[k] = (pr[k, :, 0:256] + xr[k, 0].astype(F32)) + (xr[k, 1].astype(F32) + xr[k, 2].astype(F32))
        send(("zg", k), zg.at[k, pl.ds(al((1 - h) * 128, 128), 128), :], zgr.at[k], dev(dz=2))

    def e(k):
        recv(("zg", k), zgr.at[k])
        for m in (1, 3, 2):
            recv(("yr", k, m), yr.at[k, m - 1])
        mine = pl.ds(al(h * 128, 128), 128)
        both = zg[k, mine, :] + zgr[k]
        gate, up = both[:, :128], both[:, 128:]
        back = (zb[k] + yr[k, 0].astype(F32)) + (yr[k, 1].astype(F32) + yr[k, 2].astype(F32))
        sig = jax.nn.sigmoid(gate)
        act = gate * sig
        at = pl.ds(al(k * 512 + c * 256 + h * 128, 128), 128)
        dcat[at, 0:128] = (back * up * sig * (1.0 + gate * (1.0 - sig))).astype(BF16)
        dcat[at, 128:256] = (back * act).astype(BF16)
        cols = pl.ds(al(l * 128, 128), 128)
        hid[at, cols] = (act * up).astype(BF16)
        send(("ag", k), dcat.at[at, 0:256], dcat.at[at, 0:256], dev(dz=2))
        for d in (2, 1, 3):
            send(("ah", k, d), hid.at[at, cols], hid.at[at, cols], dev(dz=d))

    def a2x(k):
        there = pl.ds(al(k * 512 + c * 256 + (1 - h) * 128, 128), 128)
        recv(("ag", k), dcat.at[there, 0:256])
        for j in (1, 3) if FWD_XG else (2, 1, 3):
            send(("xg", k, j), dcat.at[half(k, c), 0:256], dcat.at[half(k, c), pl.ds(256 * (4 - j), 256)], dev(dx=j))

    def a2y(k):
        for d in (1, 2, 3):
            zz = (z - d + 4) % 4
            at = pl.ds(al(k * 512 + c * 256 + (zz // 2) * 128, 128), 128)
            recv(("ah", k, d), hid.at[at, pl.ds(al((zz % 2) * 128, 128), 128)])
        for m in (1, 3) if FWD_YG else (2, 1, 3):
            send(("yg", k, m), hid.at[half(k, c), 0:256], hid.at[half(k, c), pl.ds(256 * (4 - m), 256)], dev(dy=m))

    def fwd_half(k, j):
        return pl.ds(al(k * 512 + c * 256 + (0 if j == 1 else 128), 128), 128)

    def af(k, on, name, buf, to):
        if on:
            for j in (1, 3):
                recv((name, k, j), buf.at[half(k, c), pl.ds(256 * (4 - j), 256)])
                send((name + "f", k, j), buf.at[fwd_half(k, j), pl.ds(256 * (4 - j), 256)], buf.at[fwd_half(k, j), pl.ds(512, 256)], to(j))

    def afx(k):
        af(k, FWD_XG, "xg", dcat, lambda j: dev(dx=j))

    def afy(k):
        af(k, FWD_YG, "yg", hid, lambda j: dev(dy=j))

    def gathered(k, on, name, buf):
        if on:
            for j in (1, 3):
                recv((name + "f", k, j), buf.at[fwd_half(k, j), pl.ds(512, 256)])
        else:
            for j in (1, 3, 2):
                recv((name, k, j), buf.at[half(k, c), pl.ds(256 * (4 - j), 256)])

    def a3(k):
        gathered(k, FWD_XG, "xg", dcat)
        send(("cg", k), dcat.at[half(k, c), :], dcat.at[half(k, c), :], dev(dc=1))

    def a4(k):
        gathered(k, FWD_YG, "yg", hid)
        send(("ch", k), hid.at[half(k, c), :], hid.at[half(k, c), :], dev(dc=1))

    def need_d(k):
        recv(("cg", k), dcat.at[half(k, 1 - c), :])

    def times_w(lhs, n):
        return lax.dot_general(
            lhs, wcat[pl.ds(al(n * 256, 256), 256), :], (((1,), (1,)), ((), ())), preferred_element_type=F32
        )

    def xk(k):
        need_d(k)
        if k in DZ:
            n_k = DZ.index(k)

            @pl.loop(0, 3)
            def _(n):
                at = pl.ds(al(n * 256, 256), 256)
                part = times_w(jnp.concatenate([dcat[half(k, 1 - l), :], dcat[half(k, l), :]], axis=0), n)
                dzs[k, :, at] = part[:256].astype(BF16)
                dxo[n_k, :, at] = part[256:]

            send(("dz", k), dzs.at[k], dzr.at[k], lpart())
        else:
            n_k = DY.index(k)

            @pl.loop(0, 3)
            def _(n):
                at = pl.ds(al(n * 256, 256), 256)
                part = times_w(dcat[pl.ds(512 * k, 512), :], n).reshape(2, 4, 64, 256)
                dxs[k, :, :, :, at] = part.astype(BF16)
                dxf[n_k, :, :, :, at] = part

            for m in (2, 1, 3):
                send(("dx", k, m), dxs.at[k, :, (y + m) % 4], dxr.at[k, m - 1], dev(dy=m))

    def x2(k):
        if k in DZ:
            n_k = DZ.index(k)
            recv(("dz", k), dzr.at[k])

            @pl.loop(0, 4)
            def _(r):
                at = pl.ds(al(r * 64, 64), 64)
                total = dxo[n_k, at, :] + dzr[k, at, :].astype(F32)
                dxo[n_k, at, :] = total
                dxs[k, 0, r] = total.astype(BF16)

            for m in (2, 1, 3):
                send(("dx", k, m), dxs.at[k, 0, (y + m) % 4], dxr.at[k, m - 1, 0], dev(dy=m))
        else:
            n_k = DY.index(k)
            for m in (1, 3, 2):
                recv(("dx", k, m), dxr.at[k, m - 1])
            total = (dxf[n_k, :, y] + dxr[k, 0].astype(F32)) + (dxr[k, 1].astype(F32) + dxr[k, 2].astype(F32))
            dxf[n_k, :, 0] = total
            dxs[k, :, y] = total.astype(BF16)
            send(("dz", k), dxs.at[k, 1 - l, y], dzr.at[k, 0:64], lpart())

    def xt(k):
        at = pl.ds(64 * k, 64)
        if k in DZ:
            for m in (1, 3, 2):
                recv(("dx", k, m), dxr.at[k, m - 1, 0])
            d_in[at, :] = (
                (dxo[DZ.index(k), pl.ds(al(y * 64, 64), 64), :] + dxr[k, 0, 0].astype(F32))
                + (dxr[k, 1, 0].astype(F32) + dxr[k, 2, 0].astype(F32))
            ).astype(BF16)
        else:
            recv(("dz", k), dzr.at[k, 0:64])
            d_in[at, :] = (dxf[DY.index(k), l, 0] + dzr[k, 0:64].astype(F32)).astype(BF16)

    def grad_part(k, n, cols):
        at = pl.ds(al(n * 256, 256), 256)
        return at, lax.dot_general(
            xin[pl.ds(512 * k, 512), at], dcat[pl.ds(512 * k, 512), cols], (((0,), (0,)), ((), ())),
            preferred_element_type=F32,
        )

    begun = []

    def gp(k):
        need_d(k)
        first = not begun
        begun.append(k)

        @pl.loop(0, 3)
        def _(n):
            @pl.loop(0, 4)
            def _(j):
                cols = pl.ds(al(j * 256, 256), 256)
                at, part = grad_part(k, n, cols)
                gacc[at, cols] = part if first else gacc[at, cols] + part

    def gf(j):
        need_d(3)
        cols = pl.ds(256 * j, 256)

        @pl.loop(0, 3)
        def _(n):
            at, part = grad_part(3, n, cols)
            gs[j, at, :] = (gacc[at, cols] + part).astype(BF16)

        here = pl.ds(al(x * 768, 256), 768)
        for q, out in enumerate((g_gate, g_up)):
            src = gs.at[j, :, pl.ds(128 * q, 128)]
            if j:
                send(("gw", j, q), src, out.at[here, :], dev(dx=j))
            else:
                move(src, out.at[here, :])

    def gd():
        for k in range(4):
            recv(("ch", k), hid.at[half(k, 1 - c), :])

        @pl.loop(0, 4)
        def _(m):
            there = (y + m) % 4
            g_down[pl.ds(al(there * 256, 256), 256), :] = lax.dot_general(
                hid[:, pl.ds(al(m * 256, 256), 256)], og[...].reshape(2048, 384), (((0,), (0,)), ((), ())),
                preferred_element_type=F32,
            ).astype(BF16)

    steps = (
        (stz, 1), (sty, 1), (st_w, 0), (st_og, -1), (sty, 0), (st_w, 1), (st_og, 1), (stz, 3), (fw, 1), (stz, 0),
        (ox, 2), (st_og, 0), (fw, 0), (b1, 1), (stz, 2), (fi, 1), (b2, 1), (sty, 3), (ox, 3), (b1, 0), (fi, 0),
        (sty, 2), (g1, 1), (b2, 0), (fw, 2), (b1, 2), (g2, 1), (fw, 3), (g1, 0), (fi, 2), (g2, 0), (b2, 2),
        (fi, 3), (b3, 1), (g1, 2), (g3, 1), (g2, 2), (g3, 0), (b3, 0), (g1, 3), (e, 1), (e, 0), (g2, 3), (b1, 3),
        (g3, 2), (a2y, 1), (b2, 3), (a2x, 0), (b3, 2), (e, 2), (afy, 1), (a2x, 1), (g3, 3), (b3, 3), (a3, 0),
        (a2x, 2), (e, 3), (a3, 1), (a2y, 2), (xk, 0), (a2y, 0), (a3, 2), (a2y, 3), (a2x, 3), (xk, 1), (xk, 2),
        (gp, 1), (gp, 2), (a3, 3), (gp, 0), (a4, 1), (afy, 3), (afy, 0), (gf, 2), (afy, 2), (xk, 3), (gf, 3),
        (x2, 0), (gf, 1), (x2, 2), (a4, 3), (a4, 2), (a4, 0), (gd,), (x2, 1), (x2, 3), (gf, 0), (xt, 0), (xt, 1),
        (xt, 2), (xt, 3),
    )
    for step in steps:
        step[0](*step[1:])

    for j in (1, 3, 2):
        for q, out in enumerate((g_gate, g_up)):
            recv(("gw", j, q), out.at[pl.ds(al(((x - j + 4) % 4) * 768, 256), 768), :])
    for copy in local[n_first:]:
        copy.wait()
    done = [id(copy) for copy in uses[:-N_SLOT]]
    for copy in sent:
        if id(copy) not in done:
            copy.wait_send()
    assert len(index) <= N_SEM, len(index)


def finish(*refs):
    ins, outs = [], []
    for k, (src, dst) in enumerate(zip(refs[:4], refs[4:8])):
        buf, n = refs[8 + k], src.shape[0] // 4
        for part in range(4):
            at = pl.ds(part * n, n)
            ins.append(pltpu.make_async_copy(src.at[at], buf.at[at], refs[12].at[len(ins)]))
            outs.append(pltpu.make_async_copy(buf.at[at], dst.at[at], refs[13].at[len(outs)]))
            ins[-1].start()
    for first, then in zip(ins, outs):
        first.wait()
        then.start()
    for then in outs:
        then.wait()


def shards(inputs, out_grad, w_gate, w_up, w_down):
    v = pltpu.VMEM
    any_ = pl.BlockSpec(memory_space=pl.ANY)
    vm = pl.BlockSpec(memory_space=pltpu.VMEM)
    outs = pl.pallas_call(
        kernel,
        name="swiglu_back",
        out_shape=(
            jax.ShapeDtypeStruct((256, 768), BF16),
            jax.ShapeDtypeStruct((3072, 128), BF16),
            jax.ShapeDtypeStruct((3072, 128), BF16),
            jax.ShapeDtypeStruct((1024, 384), BF16),
        ),
        in_specs=[any_] * 5,
        out_specs=(vm, any_, any_, vm),
        scratch_shapes=[
            v((2048, 768), BF16),
            v((768, 1024), BF16),
            v((4, 8, 4, 16, 384), BF16),
            v((1024, 384), BF16),
            v((N_SLOT, 512, 1024), F32),
            v((8, 256, 1024), F32),
            v((8, 256, 1024), BF16),
            v((4, 3, 256, 256), BF16),
            v((4, 3, 128, 128), BF16),
            v((4, 256, 256), F32),
            v((4, 128, 256), F32),
            v((4, 128, 128), F32),
            v((4, 3, 128, 512), BF16),
            v((4, 128, 512), BF16),
            v((2048, 1024), BF16),
            v((2048, 1024), BF16),
            v((4, 256, 768), BF16),
            v((4, 256, 768), BF16),
            v((max(1, len(DZ)), 256, 768), F32),
            v((max(1, len(DY)), 2, 4, 64, 768), F32),
            v((4, 2, 4, 64, 768), BF16),
            v((4, 3, 2, 64, 768), BF16),
            v((4, 768, 256), BF16),
            v((768, 1024), F32),
            pltpu.SemaphoreType.DMA((N_SEM,)),
            pltpu.SemaphoreType.DMA((N_SEM,)),
            pltpu.SemaphoreType.DMA((20,)),
        ],
        compiler_params=pltpu.CompilerParams(collective_id=0, has_side_effects=True, vmem_limit_bytes=61 * 2**20),
        cost_estimate=pl.CostEstimate(flops=13 * 10**9, bytes_accessed=8 * 2**20, transcendentals=65536),
    )(inputs, out_grad.reshape(4, 4, 16, 3072), w_gate, w_up, w_down)
    return pl.pallas_call(
        finish,
        name="results",
        out_shape=tuple(jax.ShapeDtypeStruct(v.shape, v.dtype) for v in outs),
        in_specs=[any_] * 4,
        out_specs=(any_,) * 4,
        scratch_shapes=[v(o.shape, o.dtype) for o in outs] + [pltpu.SemaphoreType.DMA((16,))] * 2,
        cost_estimate=pl.CostEstimate(flops=0, bytes_accessed=5 * 2**20, transcendentals=0),
    )(*outs)


def solution(mesh):
    in_specs = (
        P("tok", "in"),
        P("tok", "in"),
        P("in", ("out", "tok")),
        P("in", ("out", "tok")),
        P("out", ("in", "tok")),
    )
    out_specs = (
        P("tok", ("in", "out")),
        P("in", ("out", "tok")),
        P("in", ("out", "tok")),
        P("out", ("in", "tok")),
    )
    return jax.shard_map(shards, mesh=mesh, in_specs=in_specs, out_specs=out_specs, check_vma=False)
```

```python
import jax
import jax.numpy as jnp
from jax import lax
from jax.experimental import pallas as pl
from jax.experimental.pallas import tpu as pltpu
from jax.sharding import PartitionSpec as P

MESH = pl.DeviceIdType.MESH
F32 = jnp.float32
BF16 = jnp.bfloat16
N_SEM = 230
N_SLOT = 3
OX = (2, 4)
DZ = (0, 2, 3)
TILED = (3,)
DY = tuple(k for k in range(4) if k not in DZ)
Z_FIRST = (0, 1, 2, 3)
FWD_IN, FWD_XG, FWD_YG, FWD_OG = True, False, True, False


def kernel(
    inputs, out_grad, w_gate, w_up, w_down,
    d_in, g_gate, g_up, g_down,
    xin, wcat, og, wdn, pbuf, pr, s2, xr, yr, zg, zgr, zb, zbr, yb, dcat, hid, dzs, dzr, dxo, dxf, dxs, dxr, gs, gacc,
    ssem, rsem, lsem,
):
    i = lax.axis_index("in")
    x = lax.axis_index("out")
    t = lax.axis_index("tok")
    h, c, y, l = i // 2, i % 2, t // 2, t % 2
    z = 2 * h + l

    def dev(dx=0, dy=0, dz=0, dc=0):
        zz = (z + dz) % 4
        return (2 * (zz // 2) + (c + dc) % 2, (x + dx) % 4, 2 * ((y + dy) % 4) + zz % 2)

    def lpart():
        return (i, x, 2 * y + 1 - l)

    def al(v, n):
        return pl.multiple_of(v, n)

    index, sent, local, got = {}, [], [], set()

    def sem_of(key):
        if key not in index:
            index[key] = len(index)
        return index[key]

    def send(key, src, dst, device):
        n = sem_of(key)
        copy = pltpu.make_async_remote_copy(
            src_ref=src, dst_ref=dst, send_sem=ssem.at[n], recv_sem=rsem.at[n],
            device_id=device, device_id_type=MESH,
        )
        copy.start()
        sent.append(copy)
        return copy

    def recv(key, dst):
        if key in got:
            return
        got.add(key)
        n = sem_of(key)
        pltpu.make_async_remote_copy(
            src_ref=dst, dst_ref=dst, send_sem=ssem.at[n], recv_sem=rsem.at[n],
            device_id=dev(dc=1), device_id_type=MESH,
        ).wait_recv()

    def move(src, dst):
        copy = pltpu.make_async_copy(src, dst, lsem.at[len(local)])
        copy.start()
        local.append(copy)
        return copy

    def rows(s, yy, ll):
        return pl.ds(al(s * 512 + ll * 256 + yy * 64, 64), 64)

    def half(s, part):
        return pl.ds(al(s * 512 + part * 256, 256), 256)

    cols_in = pl.ds(al(x * 768, 128), 768)
    by_x = pl.ds(OX[0], OX[1] - OX[0])
    own_in = []
    for s in range(4):
        here = pl.ds(64 * s, 64)
        own_in.append(move(inputs.at[here, cols_in], xin.at[rows(s, y, l), :]))
    own_og = {}
    for s in range(4):
        if not OX[0] <= s < OX[1]:
            own_og[s] = move(out_grad.at[s, :, :, pl.ds(al(t * 384, 128), 384)], og.at[s, 4 * l + y])
    if OX[0] < OX[1]:
        own_og[-1] = move(out_grad.at[by_x, x, :, pl.ds(al(t * 384, 128), 384)], og.at[by_x, 4 * l + y, x])
    own_dn = move(w_down, wdn)
    own_w = [
        move(w.at[pl.ds(al(x * 768, 256), 768), :], wcat.at[:, pl.ds(128 * q, 128)])
        for q, w in enumerate((w_gate, w_up))
    ]
    n_first = len(local)

    barrier = pltpu.get_barrier_semaphore()
    peers = [dev(dc=1)]
    peers += [dev(dx=m) for m in (1, 2, 3)]
    peers += [dev(dy=m) for m in (1, 2, 3)]
    peers += [dev(dz=m) for m in (1, 2, 3)]
    cross = [(i, x, 2 * ((y + m) % 4) + 1 - l) for m in (1, 2, 3)]
    peers += cross
    for peer in peers:
        pl.semaphore_signal(barrier, inc=1, device_id=peer, device_id_type=MESH)
    pl.semaphore_wait(barrier, len(peers))

    def og_cols(yy, ll):
        return pl.ds(al((2 * yy + ll) * 384, 128), 384)

    def og_from(s, yy, ll):
        return og.at[s, 4 * ll + yy] if s >= 0 else og.at[by_x, 4 * ll + yy, x]

    def og_src(s, yy, ll):
        return out_grad.at[s, :, :, og_cols(yy, ll)] if s >= 0 else out_grad.at[by_x, x, :, og_cols(yy, ll)]

    def st_og(s):
        send(("og", s, 0, 1), og_src(s, y, 1 - l), og_from(s, y, l), lpart())
        for m in (2, 1, 3):
            there = (y + m) % 4
            send(("og", s, m, 0), og_src(s, there, l), og_from(s, y, l), dev(dy=m))
            send(("og", s, m, 1), og_src(s, there, 1 - l), og_from(s, y, l), cross[m - 1])

    def take_og(s):
        if s not in taken:
            own_og[s].wait()
            taken.append(s)
        recv(("og", s, 0, 1), og_from(s, y, 1 - l))
        for m in (1, 3, 2):
            yy = (y - m + 4) % 4
            recv(("og", s, m, 0), og_from(s, yy, l))
            recv(("og", s, m, 1), og_from(s, yy, 1 - l))

    taken = []

    def og_part(s, j):
        return og.at[s, :, (x + j) % 4]

    def ox(s):
        if OX[0] <= s < OX[1]:
            take_og(-1)
            for j in (1, 3) if FWD_OG else (2, 1, 3):
                send(("ox", s, j), og_part(s, 0), og_part(s, 0), dev(dx=j))

    def og_far(s, j):
        return og.at[s, pl.ds(0 if j == 1 else 4, 4), (x - j + 4) % 4]

    def fo(s):
        if FWD_OG and OX[0] <= s < OX[1]:
            for j in (1, 3):
                recv(("ox", s, j), og_part(s, 4 - j))
                send(("of", s, j), og_far(s, j), og_far(s, j), dev(dx=j))

    def wait_og(s):
        if not OX[0] <= s < OX[1]:
            take_og(s)
        elif FWD_OG:
            for j in (1, 3):
                recv(("of", s, j), og.at[s, pl.ds(0 if j == 1 else 4, 4), (x + 2) % 4])
        else:
            for j in (1, 3, 2):
                recv(("ox", s, j), og_part(s, 4 - j))

    def stz(s):
        here = pl.ds(64 * s, 64)
        at = rows(s, y, l)
        send(("in", s, 0, 1), inputs.at[here, cols_in], xin.at[at, :], lpart())

    def sty(s):
        here = pl.ds(64 * s, 64)
        at = rows(s, y, l)
        for m in (1, 3) if FWD_IN else (2, 1, 3):
            send(("in", s, m, 0), inputs.at[here, cols_in], xin.at[at, :], dev(dy=m))

    def st_w(q):
        w = (w_gate, w_up)[q]
        for j in (2, 1, 3):
            send(
                ("w", j, q), w.at[pl.ds(al(((x + j) % 4) * 768, 256), 768), :],
                wcat.at[:, pl.ds(256 * (4 - j) + 128 * q, 128)], dev(dx=j),
            )

    def part_rows(s, yy, ll, m):
        return pl.ds(al(s * 512 + ll * 256 + yy * 64 + (0 if m == 1 else 32), 32), 32)

    def fw(s):
        if s in Z_FIRST:
            at = rows(s, y, 1 - l)
            recv(("in", s, 0, 1), xin.at[at, :])
            for m in (1, 3) if FWD_IN else (2, 1, 3):
                send(("in", s, m, 1), xin.at[at, :], xin.at[at, :], dev(dy=m))

    def fi(s):
        if FWD_IN:
            for q in (0, 1) if s in Z_FIRST else (0,):
                for m in (1, 3):
                    yy, ll = (y - m + 4) % 4, (1 - l if q else l)
                    recv(("in", s, m, q), xin.at[rows(s, yy, ll), :])
                    at = part_rows(s, yy, ll, m)
                    send(("if", s, m, q), xin.at[at, :], xin.at[at, :], dev(dy=m))

    def far_in(s, q):
        yy, ll = (y + 2) % 4, (1 - l if q else l)
        if FWD_IN:
            for m in (1, 3):
                recv(("if", s, m, q), xin.at[part_rows(s, yy, ll, m), :])
        else:
            recv(("in", s, 2, q), xin.at[rows(s, yy, ll), :])

    def fz(s):
        if s not in Z_FIRST:
            for m in (1, 3, 2):
                at = rows(s, (y - m + 4) % 4, l)
                if m == 2:
                    far_in(s, 0)
                elif not FWD_IN:
                    recv(("in", s, m, 0), xin.at[at, :])
                send(("in", s, m, 1), xin.at[at, :], xin.at[at, :], lpart())

    def wait_in(s):
        own_in[s].wait()
        if s in Z_FIRST:
            if not FWD_IN:
                for m in (1, 3):
                    for q in (0, 1):
                        recv(("in", s, m, q), xin.at[rows(s, (y - m + 4) % 4, 1 - l if q else l), :])
            far_in(s, 0)
            far_in(s, 1)
        else:
            recv(("in", s, 0, 1), xin.at[rows(s, y, 1 - l), :])
            for m in (1, 3, 2):
                recv(("in", s, m, 1), xin.at[rows(s, (y - m + 4) % 4, 1 - l), :])

    uses = []

    def partial_slot():
        n = len(uses)
        if n >= N_SLOT:
            uses[n - N_SLOT].wait_send()
        return n % N_SLOT

    def core_send(slot, n):
        uses.append(send(("cr", n), pbuf.at[slot, pl.ds(al((1 - c) * 256, 256), 256), :], pr.at[n], dev(dc=1)))

    slots, seen = {}, []

    def b1(s):
        wait_og(s)
        if "dn" not in taken:
            own_dn.wait()
            taken.append("dn")
        slot = partial_slot()
        slots["b", s] = slot

        @pl.loop(0, 4)
        def _(m):
            there = (y + m) % 4
            part = lax.dot_general(
                og[s].reshape(512, 384), wdn[pl.ds(al(there * 256, 256), 256), :],
                (((1,), (1,)), ((), ())), preferred_element_type=F32,
            )
            for ll in (0, 1):
                pbuf[slot, :, pl.ds(al(ll * 512 + m * 128, 128), 128)] = part[:, 128 * ll : 128 * ll + 128]

        core_send(slot, 4 + s)

    def g1(s):
        wait_in(s)
        if "w" not in taken:
            taken.append("w")
            for copy in own_w:
                copy.wait()
            for j in (1, 3, 2):
                for q in (0, 1):
                    recv(("w", j, q), wcat.at[:, pl.ds(256 * (4 - j) + 128 * q, 128)])
        slot = partial_slot()
        slots["g", s] = slot

        @pl.loop(0, 4)
        def _(n):
            at = pl.ds(al(n * 256, 256), 256)
            pbuf[slot, :, at] = jnp.dot(xin[pl.ds(512 * s, 512), :], wcat[:, at], preferred_element_type=F32)

        core_send(slot, s)

    def core_sum(slot, n):
        recv(("cr", n), pr.at[n])

        @pl.loop(0, 8)
        def _(r):
            at = pl.ds(al(r * 32, 32), 32)
            mine = pl.ds(al(c * 256 + r * 32, 32), 32)
            total = pbuf[slot, mine, :] + pr[n, at, :]
            pr[n, at, :] = total
            s2[n, at, :] = total.astype(BF16)

    def b2(s):
        core_sum(slots["b", s], 4 + s)
        for d in (2, 1, 3):
            zz = (z + d) % 4
            at = (4 + s, pl.ds(al((zz // 2) * 128, 128), 128), pl.ds(al((zz % 2) * 512, 512), 512))
            send(("zb", s, d), s2.at[at], zbr.at[s, d - 1], dev(dz=d))

    def g2(s):
        core_sum(slots["g", s], s)
        for j in (2, 1, 3):
            send(("xr", s, j), s2.at[s, :, pl.ds(256 * j, 256)], xr.at[s, j - 1], dev(dx=j))

    def b3(k):
        for d in (1, 3, 2):
            recv(("zb", k, d), zbr.at[k, d - 1])
        mine = pr[4 + k, pl.ds(al(h * 128, 128), 128), pl.ds(al(l * 512, 512), 512)]
        total = (mine + zbr[k, 0].astype(F32)) + (zbr[k, 1].astype(F32) + zbr[k, 2].astype(F32))
        zb[k] = total[:, :128]
        yb[k] = total.astype(BF16)
        for m in (2, 1, 3):
            send(("yr", k, m), yb.at[k, :, pl.ds(128 * m, 128)], yr.at[k, m - 1], dev(dy=m))

    def g3(k):
        for j in (1, 3, 2):
            recv(("xr", k, j), xr.at[k, j - 1])
        zg[k] = (pr[k, :, 0:256] + xr[k, 0].astype(F32)) + (xr[k, 1].astype(F32) + xr[k, 2].astype(F32))
        send(("zg", k), zg.at[k, pl.ds(al((1 - h) * 128, 128), 128), :], zgr.at[k], dev(dz=2))

    def e(k):
        recv(("zg", k), zgr.at[k])
        for m in (1, 3, 2):
            recv(("yr", k, m), yr.at[k, m - 1])
        mine = pl.ds(al(h * 128, 128), 128)
        both = zg[k, mine, :] + zgr[k]
        gate, up = both[:, :128], both[:, 128:]
        back = (zb[k] + yr[k, 0].astype(F32)) + (yr[k, 1].astype(F32) + yr[k, 2].astype(F32))
        sig = jax.nn.sigmoid(gate)
        act = gate * sig
        at = pl.ds(al(k * 512 + c * 256 + h * 128, 128), 128)
        dcat[at, 0:128] = (back * up * sig * (1.0 + gate * (1.0 - sig))).astype(BF16)
        dcat[at, 128:256] = (back * act).astype(BF16)
        cols = pl.ds(al(l * 128, 128), 128)
        hid[at, cols] = (act * up).astype(BF16)
        send(("ag", k), dcat.at[at, 0:256], dcat.at[at, 0:256], dev(dz=2))
        for d in (2, 1, 3):
            send(("ah", k, d), hid.at[at, cols], hid.at[at, cols], dev(dz=d))

    def a2x(k):
        there = pl.ds(al(k * 512 + c * 256 + (1 - h) * 128, 128), 128)
        recv(("ag", k), dcat.at[there, 0:256])
        for j in (1, 3) if FWD_XG else (2, 1, 3):
            send(("xg", k, j), dcat.at[half(k, c), 0:256], dcat.at[half(k, c), pl.ds(256 * (4 - j), 256)], dev(dx=j))

    def a2y(k):
        for d in (1, 2, 3):
            zz = (z - d + 4) % 4
            at = pl.ds(al(k * 512 + c * 256 + (zz // 2) * 128, 128), 128)
            recv(("ah", k, d), hid.at[at, pl.ds(al((zz % 2) * 128, 128), 128)])
        for m in (1, 3) if FWD_YG else (2, 1, 3):
            send(("yg", k, m), hid.at[half(k, c), 0:256], hid.at[half(k, c), pl.ds(256 * (4 - m), 256)], dev(dy=m))

    def fwd_half(k, j):
        return pl.ds(al(k * 512 + c * 256 + (0 if j == 1 else 128), 128), 128)

    def af(k, on, name, buf, to):
        if on:
            for j in (1, 3):
                recv((name, k, j), buf.at[half(k, c), pl.ds(256 * (4 - j), 256)])
                send((name + "f", k, j), buf.at[fwd_half(k, j), pl.ds(256 * (4 - j), 256)], buf.at[fwd_half(k, j), pl.ds(512, 256)], to(j))

    def afx(k):
        af(k, FWD_XG, "xg", dcat, lambda j: dev(dx=j))

    def afy(k):
        af(k, FWD_YG, "yg", hid, lambda j: dev(dy=j))

    def gathered(k, on, name, buf):
        if on:
            for j in (1, 3):
                recv((name + "f", k, j), buf.at[fwd_half(k, j), pl.ds(512, 256)])
        else:
            for j in (1, 3, 2):
                recv((name, k, j), buf.at[half(k, c), pl.ds(256 * (4 - j), 256)])

    def a3(k):
        gathered(k, FWD_XG, "xg", dcat)
        send(("cg", k), dcat.at[half(k, c), :], dcat.at[half(k, c), :], dev(dc=1))

    def a4(k):
        gathered(k, FWD_YG, "yg", hid)
        send(("ch", k), hid.at[half(k, c), :], hid.at[half(k, c), :], dev(dc=1))

    def need_d(k):
        recv(("cg", k), dcat.at[half(k, 1 - c), :])

    def times_w(lhs, n):
        return lax.dot_general(
            lhs, wcat[pl.ds(al(n * 256, 256), 256), :], (((1,), (1,)), ((), ())), preferred_element_type=F32
        )

    def xk(k):
        need_d(k)
        if k in TILED:
            for n in range(3):
                at = pl.ds(256 * n, 256)
                part = times_w(jnp.concatenate([dcat[half(k, 1 - l), :], dcat[half(k, l), :]], axis=0), n)
                dzs[k, :, at] = part[:256].astype(BF16)
                send(("dz", k, n), dzs.at[k, :, at], dzr.at[k, :, at], lpart())
                dxo[DZ.index(k), :, at] = part[256:]
        elif k in DZ:
            n_k = DZ.index(k)

            @pl.loop(0, 3)
            def _(n):
                at = pl.ds(al(n * 256, 256), 256)
                part = times_w(jnp.concatenate([dcat[half(k, 1 - l), :], dcat[half(k, l), :]], axis=0), n)
                dzs[k, :, at] = part[:256].astype(BF16)
                dxo[n_k, :, at] = part[256:]

            send(("dz", k), dzs.at[k], dzr.at[k], lpart())
        else:
            n_k = DY.index(k)

            @pl.loop(0, 3)
            def _(n):
                at = pl.ds(al(n * 256, 256), 256)
                part = times_w(dcat[pl.ds(512 * k, 512), :], n).reshape(2, 4, 64, 256)
                dxs[k, :, :, :, at] = part.astype(BF16)
                dxf[n_k, :, :, :, at] = part

            for m in (2, 1, 3):
                send(("dx", k, m), dxs.at[k, :, (y + m) % 4], dxr.at[k, m - 1], dev(dy=m))

    def x2(k):
        if k in TILED:
            n_k = DZ.index(k)
            for n in range(3):
                cols = pl.ds(256 * n, 256)
                recv(("dz", k, n), dzr.at[k, :, cols])
                total = dxo[n_k, :, cols] + dzr[k, :, cols].astype(F32)
                dxo[n_k, :, cols] = total
                dxs[k, 0, :, :, cols] = total.astype(BF16).reshape(4, 64, 256)
                for m in (2, 1, 3):
                    send(
                        ("dx", k, m, n), dxs.at[k, 0, (y + m) % 4, :, cols], dxr.at[k, m - 1, 0, :, cols], dev(dy=m)
                    )
        elif k in DZ:
            n_k = DZ.index(k)
            recv(("dz", k), dzr.at[k])

            @pl.loop(0, 4)
            def _(r):
                at = pl.ds(al(r * 64, 64), 64)
                total = dxo[n_k, at, :] + dzr[k, at, :].astype(F32)
                dxo[n_k, at, :] = total
                dxs[k, 0, r] = total.astype(BF16)

            for m in (2, 1, 3):
                send(("dx", k, m), dxs.at[k, 0, (y + m) % 4], dxr.at[k, m - 1, 0], dev(dy=m))
        else:
            n_k = DY.index(k)
            for m in (1, 3, 2):
                recv(("dx", k, m), dxr.at[k, m - 1])
            total = (dxf[n_k, :, y] + dxr[k, 0].astype(F32)) + (dxr[k, 1].astype(F32) + dxr[k, 2].astype(F32))
            dxf[n_k, :, 0] = total
            dxs[k, :, y] = total.astype(BF16)
            send(("dz", k), dxs.at[k, 1 - l, y], dzr.at[k, 0:64], lpart())

    def xt(k):
        at = pl.ds(64 * k, 64)
        if k in DZ:
            for m in (1, 3, 2):
                if k in TILED:
                    for n in range(3):
                        recv(("dx", k, m, n), dxr.at[k, m - 1, 0, :, pl.ds(256 * n, 256)])
                else:
                    recv(("dx", k, m), dxr.at[k, m - 1, 0])
            d_in[at, :] = (
                (dxo[DZ.index(k), pl.ds(al(y * 64, 64), 64), :] + dxr[k, 0, 0].astype(F32))
                + (dxr[k, 1, 0].astype(F32) + dxr[k, 2, 0].astype(F32))
            ).astype(BF16)
        else:
            recv(("dz", k), dzr.at[k, 0:64])
            d_in[at, :] = (dxf[DY.index(k), l, 0] + dzr[k, 0:64].astype(F32)).astype(BF16)

    def grad_part(k, n, cols):
        at = pl.ds(al(n * 256, 256), 256)
        return at, lax.dot_general(
            xin[pl.ds(512 * k, 512), at], dcat[pl.ds(512 * k, 512), cols], (((0,), (0,)), ((), ())),
            preferred_element_type=F32,
        )

    begun = []

    def gp(k):
        need_d(k)
        first = not begun
        begun.append(k)

        @pl.loop(0, 3)
        def _(n):
            @pl.loop(0, 4)
            def _(j):
                cols = pl.ds(al(j * 256, 256), 256)
                at, part = grad_part(k, n, cols)
                gacc[at, cols] = part if first else gacc[at, cols] + part

    def gf(j):
        need_d(3)
        cols = pl.ds(256 * j, 256)

        @pl.loop(0, 3)
        def _(n):
            at, part = grad_part(3, n, cols)
            gs[j, at, :] = (gacc[at, cols] + part).astype(BF16)

        here = pl.ds(al(x * 768, 256), 768)
        for q, out in enumerate((g_gate, g_up)):
            src = gs.at[j, :, pl.ds(128 * q, 128)]
            if j:
                send(("gw", j, q), src, out.at[here, :], dev(dx=j))
            else:
                move(src, out.at[here, :])

    def gd():
        for k in range(4):
            recv(("ch", k), hid.at[half(k, 1 - c), :])

        @pl.loop(0, 4)
        def _(m):
            there = (y + m) % 4
            g_down[pl.ds(al(there * 256, 256), 256), :] = lax.dot_general(
                hid[:, pl.ds(al(m * 256, 256), 256)], og[...].reshape(2048, 384), (((0,), (0,)), ((), ())),
                preferred_element_type=F32,
            ).astype(BF16)

    steps = (
        (stz, 1), (st_og, -1), (st_w, 0), (st_og, 0), (sty, 1), (fw, 1), (stz, 2), (ox, 3), (st_og, 1), (stz, 3),
        (st_w, 1), (sty, 0), (fw, 2), (fi, 1), (stz, 0), (b1, 0), (b1, 1), (fw, 3), (b2, 0), (fw, 0), (b1, 3),
        (sty, 2), (ox, 2), (g1, 1), (b2, 1), (b2, 3), (fi, 0), (g2, 1), (sty, 3), (fi, 2), (b1, 2), (g1, 0),
        (fi, 3), (b2, 2), (g2, 0), (g1, 2), (b3, 1), (g3, 1), (g1, 3), (g2, 2), (g3, 0), (g2, 3), (b3, 0),
        (e, 1), (b3, 3), (e, 0), (b3, 2), (a2x, 1), (g3, 2), (a2y, 1), (g3, 3), (a2x, 0), (e, 2), (afy, 1),
        (a3, 1), (a2x, 2), (a2y, 2), (a2y, 0), (e, 3), (a4, 1), (a3, 0), (xk, 1), (xk, 0), (a2x, 3), (a3, 2),
        (gp, 1), (a2y, 3), (xk, 2), (gp, 2), (a3, 3), (gp, 0), (x2, 0), (gf, 2), (afy, 0), (gf, 1), (afy, 2),
        (afy, 3), (gf, 3), (xk, 3), (x2, 2), (a4, 3), (x2, 1), (a4, 2), (a4, 0), (x2, 3), (gd,), (xt, 2),
        (xt, 0), (xt, 1), (gf, 0), (xt, 3),
    )
    for step in steps:
        step[0](*step[1:])

    for j in (1, 3, 2):
        for q, out in enumerate((g_gate, g_up)):
            recv(("gw", j, q), out.at[pl.ds(al(((x - j + 4) % 4) * 768, 256), 768), :])
    for copy in local[n_first:]:
        copy.wait()
    done = [id(copy) for copy in uses[:-N_SLOT]]
    for copy in sent:
        if id(copy) not in done:
            copy.wait_send()
    assert len(index) <= N_SEM, len(index)


def finish(*refs):
    ins, outs = [], []
    for k, (src, dst) in enumerate(zip(refs[:4], refs[4:8])):
        buf, n = refs[8 + k], src.shape[0] // 4
        for part in range(4):
            at = pl.ds(part * n, n)
            ins.append(pltpu.make_async_copy(src.at[at], buf.at[at], refs[12].at[len(ins)]))
            outs.append(pltpu.make_async_copy(buf.at[at], dst.at[at], refs[13].at[len(outs)]))
            ins[-1].start()
    for first, then in zip(ins, outs):
        first.wait()
        then.start()
    for then in outs:
        then.wait()


def shards(inputs, out_grad, w_gate, w_up, w_down):
    v = pltpu.VMEM
    any_ = pl.BlockSpec(memory_space=pl.ANY)
    vm = pl.BlockSpec(memory_space=pltpu.VMEM)
    outs = pl.pallas_call(
        kernel,
        name="swiglu_back",
        out_shape=(
            jax.ShapeDtypeStruct((256, 768), BF16),
            jax.ShapeDtypeStruct((3072, 128), BF16),
            jax.ShapeDtypeStruct((3072, 128), BF16),
            jax.ShapeDtypeStruct((1024, 384), BF16),
        ),
        in_specs=[any_] * 5,
        out_specs=(vm, any_, any_, vm),
        scratch_shapes=[
            v((2048, 768), BF16),
            v((768, 1024), BF16),
            v((4, 8, 4, 16, 384), BF16),
            v((1024, 384), BF16),
            v((N_SLOT, 512, 1024), F32),
            v((8, 256, 1024), F32),
            v((8, 256, 1024), BF16),
            v((4, 3, 256, 256), BF16),
            v((4, 3, 128, 128), BF16),
            v((4, 256, 256), F32),
            v((4, 128, 256), F32),
            v((4, 128, 128), F32),
            v((4, 3, 128, 512), BF16),
            v((4, 128, 512), BF16),
            v((2048, 1024), BF16),
            v((2048, 1024), BF16),
            v((4, 256, 768), BF16),
            v((4, 256, 768), BF16),
            v((max(1, len(DZ)), 256, 768), F32),
            v((max(1, len(DY)), 2, 4, 64, 768), F32),
            v((4, 2, 4, 64, 768), BF16),
            v((4, 3, 2, 64, 768), BF16),
            v((4, 768, 256), BF16),
            v((768, 1024), F32),
            pltpu.SemaphoreType.DMA((N_SEM,)),
            pltpu.SemaphoreType.DMA((N_SEM,)),
            pltpu.SemaphoreType.DMA((20,)),
        ],
        compiler_params=pltpu.CompilerParams(collective_id=0, has_side_effects=True, vmem_limit_bytes=61 * 2**20),
        cost_estimate=pl.CostEstimate(flops=13 * 10**9, bytes_accessed=8 * 2**20, transcendentals=65536),
    )(inputs, out_grad.reshape(4, 4, 16, 3072), w_gate, w_up, w_down)
    return pl.pallas_call(
        finish,
        name="results",
        out_shape=tuple(jax.ShapeDtypeStruct(v.shape, v.dtype) for v in outs),
        in_specs=[any_] * 4,
        out_specs=(any_,) * 4,
        scratch_shapes=[v(o.shape, o.dtype) for o in outs] + [pltpu.SemaphoreType.DMA((16,))] * 2,
        cost_estimate=pl.CostEstimate(flops=0, bytes_accessed=5 * 2**20, transcendentals=0),
    )(*outs)


def solution(mesh):
    in_specs = (
        P("tok", "in"),
        P("tok", "in"),
        P("in", ("out", "tok")),
        P("in", ("out", "tok")),
        P("out", ("in", "tok")),
    )
    out_specs = (
        P("tok", ("in", "out")),
        P("in", ("out", "tok")),
        P("in", ("out", "tok")),
        P("out", ("in", "tok")),
    )
    return jax.shard_map(shards, mesh=mesh, in_specs=in_specs, out_specs=out_specs, check_vma=False)
```

```python
import jax
import jax.numpy as jnp
from jax import lax
from jax.experimental import pallas as pl
from jax.experimental.pallas import tpu as pltpu
from jax.sharding import PartitionSpec as P

MESH = pl.DeviceIdType.MESH
F32 = jnp.float32
BF16 = jnp.bfloat16
N_SEM = 230
N_SLOT = 3
OX = (2, 4)
DZ = (0, 2, 3)
TILED = (3,)
DY = tuple(k for k in range(4) if k not in DZ)
Z_FIRST = (0, 1, 2, 3)
FWD_IN, FWD_XG, FWD_YG, FWD_OG = True, False, True, False


def kernel(
    inputs, out_grad, w_gate, w_up, w_down,
    d_out, g_gate, g_up, g_out,
    xin, wcat, og, wdn, pbuf, pr, s2, xr, yr, zg, zgr, zb, zbr, yb, dcat, hid, dzs, dzr, dxo, dxf, dxs, dxr, gs, gacc, d_in, g_down,
    ssem, rsem, lsem,
):
    i = lax.axis_index("in")
    x = lax.axis_index("out")
    t = lax.axis_index("tok")
    h, c, y, l = i // 2, i % 2, t // 2, t % 2
    z = 2 * h + l

    def dev(dx=0, dy=0, dz=0, dc=0):
        zz = (z + dz) % 4
        return (2 * (zz // 2) + (c + dc) % 2, (x + dx) % 4, 2 * ((y + dy) % 4) + zz % 2)

    def lpart():
        return (i, x, 2 * y + 1 - l)

    def al(v, n):
        return pl.multiple_of(v, n)

    index, sent, local, got = {}, [], [], set()

    def sem_of(key):
        if key not in index:
            index[key] = len(index)
        return index[key]

    def send(key, src, dst, device):
        n = sem_of(key)
        copy = pltpu.make_async_remote_copy(
            src_ref=src, dst_ref=dst, send_sem=ssem.at[n], recv_sem=rsem.at[n],
            device_id=device, device_id_type=MESH,
        )
        copy.start()
        sent.append(copy)
        return copy

    def recv(key, dst):
        if key in got:
            return
        got.add(key)
        n = sem_of(key)
        pltpu.make_async_remote_copy(
            src_ref=dst, dst_ref=dst, send_sem=ssem.at[n], recv_sem=rsem.at[n],
            device_id=dev(dc=1), device_id_type=MESH,
        ).wait_recv()

    def move(src, dst):
        copy = pltpu.make_async_copy(src, dst, lsem.at[len(local)])
        copy.start()
        local.append(copy)
        return copy

    def rows(s, yy, ll):
        return pl.ds(al(s * 512 + ll * 256 + yy * 64, 64), 64)

    def half(s, part):
        return pl.ds(al(s * 512 + part * 256, 256), 256)

    cols_in = pl.ds(al(x * 768, 128), 768)
    by_x = pl.ds(OX[0], OX[1] - OX[0])
    own_in = []
    for s in range(4):
        here = pl.ds(64 * s, 64)
        own_in.append(move(inputs.at[here, cols_in], xin.at[rows(s, y, l), :]))
    own_og = {}
    for s in range(4):
        if not OX[0] <= s < OX[1]:
            own_og[s] = move(out_grad.at[s, :, :, pl.ds(al(t * 384, 128), 384)], og.at[s, 4 * l + y])
    if OX[0] < OX[1]:
        own_og[-1] = move(out_grad.at[by_x, x, :, pl.ds(al(t * 384, 128), 384)], og.at[by_x, 4 * l + y, x])
    own_dn = move(w_down, wdn)
    own_w = [
        move(w.at[pl.ds(al(x * 768, 256), 768), :], wcat.at[:, pl.ds(128 * q, 128)])
        for q, w in enumerate((w_gate, w_up))
    ]
    n_first = len(local)

    barrier = pltpu.get_barrier_semaphore()
    peers = [dev(dc=1)]
    peers += [dev(dx=m) for m in (1, 2, 3)]
    peers += [dev(dy=m) for m in (1, 2, 3)]
    peers += [dev(dz=m) for m in (1, 2, 3)]
    cross = [(i, x, 2 * ((y + m) % 4) + 1 - l) for m in (1, 2, 3)]
    peers += cross
    for peer in peers:
        pl.semaphore_signal(barrier, inc=1, device_id=peer, device_id_type=MESH)
    pl.semaphore_wait(barrier, len(peers))

    def og_cols(yy, ll):
        return pl.ds(al((2 * yy + ll) * 384, 128), 384)

    def og_from(s, yy, ll):
        return og.at[s, 4 * ll + yy] if s >= 0 else og.at[by_x, 4 * ll + yy, x]

    def og_src(s, yy, ll):
        return out_grad.at[s, :, :, og_cols(yy, ll)] if s >= 0 else out_grad.at[by_x, x, :, og_cols(yy, ll)]

    def st_og(s):
        send(("og", s, 0, 1), og_src(s, y, 1 - l), og_from(s, y, l), lpart())
        for m in (2, 1, 3):
            there = (y + m) % 4
            send(("og", s, m, 0), og_src(s, there, l), og_from(s, y, l), dev(dy=m))
            send(("og", s, m, 1), og_src(s, there, 1 - l), og_from(s, y, l), cross[m - 1])

    def take_og(s):
        if s not in taken:
            own_og[s].wait()
            taken.append(s)
        recv(("og", s, 0, 1), og_from(s, y, 1 - l))
        for m in (1, 3, 2):
            yy = (y - m + 4) % 4
            recv(("og", s, m, 0), og_from(s, yy, l))
            recv(("og", s, m, 1), og_from(s, yy, 1 - l))

    taken = []

    def og_part(s, j):
        return og.at[s, :, (x + j) % 4]

    def ox(s):
        if OX[0] <= s < OX[1]:
            take_og(-1)
            for j in (1, 3) if FWD_OG else (2, 1, 3):
                send(("ox", s, j), og_part(s, 0), og_part(s, 0), dev(dx=j))

    def og_far(s, j):
        return og.at[s, pl.ds(0 if j == 1 else 4, 4), (x - j + 4) % 4]

    def fo(s):
        if FWD_OG and OX[0] <= s < OX[1]:
            for j in (1, 3):
                recv(("ox", s, j), og_part(s, 4 - j))
                send(("of", s, j), og_far(s, j), og_far(s, j), dev(dx=j))

    def wait_og(s):
        if not OX[0] <= s < OX[1]:
            take_og(s)
        elif FWD_OG:
            for j in (1, 3):
                recv(("of", s, j), og.at[s, pl.ds(0 if j == 1 else 4, 4), (x + 2) % 4])
        else:
            for j in (1, 3, 2):
                recv(("ox", s, j), og_part(s, 4 - j))

    def stz(s):
        here = pl.ds(64 * s, 64)
        at = rows(s, y, l)
        send(("in", s, 0, 1), inputs.at[here, cols_in], xin.at[at, :], lpart())

    def sty(s):
        here = pl.ds(64 * s, 64)
        at = rows(s, y, l)
        for m in (1, 3) if FWD_IN else (2, 1, 3):
            send(("in", s, m, 0), inputs.at[here, cols_in], xin.at[at, :], dev(dy=m))

    def st_w(q):
        w = (w_gate, w_up)[q]
        for j in (2, 1, 3):
            send(
                ("w", j, q), w.at[pl.ds(al(((x + j) % 4) * 768, 256), 768), :],
                wcat.at[:, pl.ds(256 * (4 - j) + 128 * q, 128)], dev(dx=j),
            )

    def part_rows(s, yy, ll, m):
        return pl.ds(al(s * 512 + ll * 256 + yy * 64 + (0 if m == 1 else 32), 32), 32)

    def fw(s):
        if s in Z_FIRST:
            at = rows(s, y, 1 - l)
            recv(("in", s, 0, 1), xin.at[at, :])
            for m in (1, 3) if FWD_IN else (2, 1, 3):
                send(("in", s, m, 1), xin.at[at, :], xin.at[at, :], dev(dy=m))

    def fi(s):
        if FWD_IN:
            for q in (0, 1) if s in Z_FIRST else (0,):
                for m in (1, 3):
                    yy, ll = (y - m + 4) % 4, (1 - l if q else l)
                    recv(("in", s, m, q), xin.at[rows(s, yy, ll), :])
                    at = part_rows(s, yy, ll, m)
                    send(("if", s, m, q), xin.at[at, :], xin.at[at, :], dev(dy=m))

    def far_in(s, q):
        yy, ll = (y + 2) % 4, (1 - l if q else l)
        if FWD_IN:
            for m in (1, 3):
                recv(("if", s, m, q), xin.at[part_rows(s, yy, ll, m), :])
        else:
            recv(("in", s, 2, q), xin.at[rows(s, yy, ll), :])

    def fz(s):
        if s not in Z_FIRST:
            for m in (1, 3, 2):
                at = rows(s, (y - m + 4) % 4, l)
                if m == 2:
                    far_in(s, 0)
                elif not FWD_IN:
                    recv(("in", s, m, 0), xin.at[at, :])
                send(("in", s, m, 1), xin.at[at, :], xin.at[at, :], lpart())

    def wait_in(s):
        own_in[s].wait()
        if s in Z_FIRST:
            if not FWD_IN:
                for m in (1, 3):
                    for q in (0, 1):
                        recv(("in", s, m, q), xin.at[rows(s, (y - m + 4) % 4, 1 - l if q else l), :])
            far_in(s, 0)
            far_in(s, 1)
        else:
            recv(("in", s, 0, 1), xin.at[rows(s, y, 1 - l), :])
            for m in (1, 3, 2):
                recv(("in", s, m, 1), xin.at[rows(s, (y - m + 4) % 4, 1 - l), :])

    uses = []

    def partial_slot():
        n = len(uses)
        if n >= N_SLOT:
            uses[n - N_SLOT].wait_send()
        return n % N_SLOT

    def core_send(slot, n):
        uses.append(send(("cr", n), pbuf.at[slot, pl.ds(al((1 - c) * 256, 256), 256), :], pr.at[n], dev(dc=1)))

    slots, seen = {}, []

    def b1(s):
        wait_og(s)
        if "dn" not in taken:
            own_dn.wait()
            taken.append("dn")
        slot = partial_slot()
        slots["b", s] = slot

        @pl.loop(0, 4)
        def _(m):
            there = (y + m) % 4
            part = lax.dot_general(
                og[s].reshape(512, 384), wdn[pl.ds(al(there * 256, 256), 256), :],
                (((1,), (1,)), ((), ())), preferred_element_type=F32,
            )
            for ll in (0, 1):
                pbuf[slot, :, pl.ds(al(ll * 512 + m * 128, 128), 128)] = part[:, 128 * ll : 128 * ll + 128]

        core_send(slot, 4 + s)

    def g1(s):
        wait_in(s)
        if "w" not in taken:
            taken.append("w")
            for copy in own_w:
                copy.wait()
            for j in (1, 3, 2):
                for q in (0, 1):
                    recv(("w", j, q), wcat.at[:, pl.ds(256 * (4 - j) + 128 * q, 128)])
        slot = partial_slot()
        slots["g", s] = slot

        @pl.loop(0, 4)
        def _(n):
            at = pl.ds(al(n * 256, 256), 256)
            pbuf[slot, :, at] = jnp.dot(xin[pl.ds(512 * s, 512), :], wcat[:, at], preferred_element_type=F32)

        core_send(slot, s)

    def core_sum(slot, n):
        recv(("cr", n), pr.at[n])

        @pl.loop(0, 8)
        def _(r):
            at = pl.ds(al(r * 32, 32), 32)
            mine = pl.ds(al(c * 256 + r * 32, 32), 32)
            total = pbuf[slot, mine, :] + pr[n, at, :]
            pr[n, at, :] = total
            s2[n, at, :] = total.astype(BF16)

    def b2(s):
        core_sum(slots["b", s], 4 + s)
        for d in (2, 1, 3):
            zz = (z + d) % 4
            at = (4 + s, pl.ds(al((zz // 2) * 128, 128), 128), pl.ds(al((zz % 2) * 512, 512), 512))
            send(("zb", s, d), s2.at[at], zbr.at[s, d - 1], dev(dz=d))

    def g2(s):
        core_sum(slots["g", s], s)
        for j in (2, 1, 3):
            send(("xr", s, j), s2.at[s, :, pl.ds(256 * j, 256)], xr.at[s, j - 1], dev(dx=j))

    def b3(k):
        for d in (1, 3, 2):
            recv(("zb", k, d), zbr.at[k, d - 1])
        mine = pr[4 + k, pl.ds(al(h * 128, 128), 128), pl.ds(al(l * 512, 512), 512)]
        total = (mine + zbr[k, 0].astype(F32)) + (zbr[k, 1].astype(F32) + zbr[k, 2].astype(F32))
        zb[k] = total[:, :128]
        yb[k] = total.astype(BF16)
        for m in (2, 1, 3):
            send(("yr", k, m), yb.at[k, :, pl.ds(128 * m, 128)], yr.at[k, m - 1], dev(dy=m))

    def g3(k):
        for j in (1, 3, 2):
            recv(("xr", k, j), xr.at[k, j - 1])
        zg[k] = (pr[k, :, 0:256] + xr[k, 0].astype(F32)) + (xr[k, 1].astype(F32) + xr[k, 2].astype(F32))
        send(("zg", k), zg.at[k, pl.ds(al((1 - h) * 128, 128), 128), :], zgr.at[k], dev(dz=2))

    def e(k):
        recv(("zg", k), zgr.at[k])
        for m in (1, 3, 2):
            recv(("yr", k, m), yr.at[k, m - 1])
        mine = pl.ds(al(h * 128, 128), 128)
        both = zg[k, mine, :] + zgr[k]
        gate, up = both[:, :128], both[:, 128:]
        back = (zb[k] + yr[k, 0].astype(F32)) + (yr[k, 1].astype(F32) + yr[k, 2].astype(F32))
        sig = jax.nn.sigmoid(gate)
        act = gate * sig
        at = pl.ds(al(k * 512 + c * 256 + h * 128, 128), 128)
        dcat[at, 0:128] = (back * up * sig * (1.0 + gate * (1.0 - sig))).astype(BF16)
        dcat[at, 128:256] = (back * act).astype(BF16)
        cols = pl.ds(al(l * 128, 128), 128)
        hid[at, cols] = (act * up).astype(BF16)
        send(("ag", k), dcat.at[at, 0:256], dcat.at[at, 0:256], dev(dz=2))
        for d in (2, 1, 3):
            send(("ah", k, d), hid.at[at, cols], hid.at[at, cols], dev(dz=d))

    def a2x(k):
        there = pl.ds(al(k * 512 + c * 256 + (1 - h) * 128, 128), 128)
        recv(("ag", k), dcat.at[there, 0:256])
        for j in (1, 3) if FWD_XG else (2, 1, 3):
            send(("xg", k, j), dcat.at[half(k, c), 0:256], dcat.at[half(k, c), pl.ds(256 * (4 - j), 256)], dev(dx=j))

    def a2y(k):
        for d in (1, 2, 3):
            zz = (z - d + 4) % 4
            at = pl.ds(al(k * 512 + c * 256 + (zz // 2) * 128, 128), 128)
            recv(("ah", k, d), hid.at[at, pl.ds(al((zz % 2) * 128, 128), 128)])
        for m in (1, 3) if FWD_YG else (2, 1, 3):
            send(("yg", k, m), hid.at[half(k, c), 0:256], hid.at[half(k, c), pl.ds(256 * (4 - m), 256)], dev(dy=m))

    def fwd_half(k, j):
        return pl.ds(al(k * 512 + c * 256 + (0 if j == 1 else 128), 128), 128)

    def af(k, on, name, buf, to):
        if on:
            for j in (1, 3):
                recv((name, k, j), buf.at[half(k, c), pl.ds(256 * (4 - j), 256)])
                send((name + "f", k, j), buf.at[fwd_half(k, j), pl.ds(256 * (4 - j), 256)], buf.at[fwd_half(k, j), pl.ds(512, 256)], to(j))

    def afx(k):
        af(k, FWD_XG, "xg", dcat, lambda j: dev(dx=j))

    def afy(k):
        af(k, FWD_YG, "yg", hid, lambda j: dev(dy=j))

    def gathered(k, on, name, buf):
        if on:
            for j in (1, 3):
                recv((name + "f", k, j), buf.at[fwd_half(k, j), pl.ds(512, 256)])
        else:
            for j in (1, 3, 2):
                recv((name, k, j), buf.at[half(k, c), pl.ds(256 * (4 - j), 256)])

    def a3(k):
        gathered(k, FWD_XG, "xg", dcat)
        send(("cg", k), dcat.at[half(k, c), :], dcat.at[half(k, c), :], dev(dc=1))

    def a4(k):
        gathered(k, FWD_YG, "yg", hid)
        send(("ch", k), hid.at[half(k, c), :], hid.at[half(k, c), :], dev(dc=1))

    def need_d(k):
        recv(("cg", k), dcat.at[half(k, 1 - c), :])

    def times_w(lhs, n):
        return lax.dot_general(
            lhs, wcat[pl.ds(al(n * 256, 256), 256), :], (((1,), (1,)), ((), ())), preferred_element_type=F32
        )

    def xk(k):
        need_d(k)
        if k in TILED:
            for n in range(3):
                at = pl.ds(256 * n, 256)
                part = times_w(jnp.concatenate([dcat[half(k, 1 - l), :], dcat[half(k, l), :]], axis=0), n)
                dzs[k, :, at] = part[:256].astype(BF16)
                send(("dz", k, n), dzs.at[k, :, at], dzr.at[k, :, at], lpart())
                dxo[DZ.index(k), :, at] = part[256:]
        elif k in DZ:
            n_k = DZ.index(k)

            @pl.loop(0, 3)
            def _(n):
                at = pl.ds(al(n * 256, 256), 256)
                part = times_w(jnp.concatenate([dcat[half(k, 1 - l), :], dcat[half(k, l), :]], axis=0), n)
                dzs[k, :, at] = part[:256].astype(BF16)
                dxo[n_k, :, at] = part[256:]

            send(("dz", k), dzs.at[k], dzr.at[k], lpart())
        else:
            n_k = DY.index(k)

            @pl.loop(0, 3)
            def _(n):
                at = pl.ds(al(n * 256, 256), 256)
                part = times_w(dcat[pl.ds(512 * k, 512), :], n).reshape(2, 4, 64, 256)
                dxs[k, :, :, :, at] = part.astype(BF16)
                dxf[n_k, :, :, :, at] = part

            for m in (2, 1, 3):
                send(("dx", k, m), dxs.at[k, :, (y + m) % 4], dxr.at[k, m - 1], dev(dy=m))

    def x2(k):
        if k in TILED:
            n_k = DZ.index(k)
            for n in range(3):
                cols = pl.ds(256 * n, 256)
                recv(("dz", k, n), dzr.at[k, :, cols])
                total = dxo[n_k, :, cols] + dzr[k, :, cols].astype(F32)
                dxo[n_k, :, cols] = total
                dxs[k, 0, :, :, cols] = total.astype(BF16).reshape(4, 64, 256)
                for m in (2, 1, 3):
                    send(
                        ("dx", k, m, n), dxs.at[k, 0, (y + m) % 4, :, cols], dxr.at[k, m - 1, 0, :, cols], dev(dy=m)
                    )
        elif k in DZ:
            n_k = DZ.index(k)
            recv(("dz", k), dzr.at[k])

            @pl.loop(0, 4)
            def _(r):
                at = pl.ds(al(r * 64, 64), 64)
                total = dxo[n_k, at, :] + dzr[k, at, :].astype(F32)
                dxo[n_k, at, :] = total
                dxs[k, 0, r] = total.astype(BF16)

            for m in (2, 1, 3):
                send(("dx", k, m), dxs.at[k, 0, (y + m) % 4], dxr.at[k, m - 1, 0], dev(dy=m))
        else:
            n_k = DY.index(k)
            for m in (1, 3, 2):
                recv(("dx", k, m), dxr.at[k, m - 1])
            total = (dxf[n_k, :, y] + dxr[k, 0].astype(F32)) + (dxr[k, 1].astype(F32) + dxr[k, 2].astype(F32))
            dxf[n_k, :, 0] = total
            dxs[k, :, y] = total.astype(BF16)
            send(("dz", k), dxs.at[k, 1 - l, y], dzr.at[k, 0:64], lpart())

    def xt(k):
        at = pl.ds(64 * k, 64)
        if k in DZ:
            for m in (1, 3, 2):
                if k in TILED:
                    for n in range(3):
                        recv(("dx", k, m, n), dxr.at[k, m - 1, 0, :, pl.ds(256 * n, 256)])
                else:
                    recv(("dx", k, m), dxr.at[k, m - 1, 0])
            d_in[at, :] = (
                (dxo[DZ.index(k), pl.ds(al(y * 64, 64), 64), :] + dxr[k, 0, 0].astype(F32))
                + (dxr[k, 1, 0].astype(F32) + dxr[k, 2, 0].astype(F32))
            ).astype(BF16)
        else:
            recv(("dz", k), dzr.at[k, 0:64])
            d_in[at, :] = (dxf[DY.index(k), l, 0] + dzr[k, 0:64].astype(F32)).astype(BF16)
        move(d_in.at[at, :], d_out.at[at, :])

    def grad_part(k, n, cols):
        at = pl.ds(al(n * 256, 256), 256)
        return at, lax.dot_general(
            xin[pl.ds(512 * k, 512), at], dcat[pl.ds(512 * k, 512), cols], (((0,), (0,)), ((), ())),
            preferred_element_type=F32,
        )

    begun = []

    def gp(k):
        need_d(k)
        first = not begun
        begun.append(k)

        @pl.loop(0, 3)
        def _(n):
            @pl.loop(0, 4)
            def _(j):
                cols = pl.ds(al(j * 256, 256), 256)
                at, part = grad_part(k, n, cols)
                gacc[at, cols] = part if first else gacc[at, cols] + part

    def gf(j):
        need_d(3)
        cols = pl.ds(256 * j, 256)

        @pl.loop(0, 3)
        def _(n):
            at, part = grad_part(3, n, cols)
            gs[j, at, :] = (gacc[at, cols] + part).astype(BF16)

        here = pl.ds(al(x * 768, 256), 768)
        for q, out in enumerate((g_gate, g_up)):
            src = gs.at[j, :, pl.ds(128 * q, 128)]
            if j:
                send(("gw", j, q), src, out.at[here, :], dev(dx=j))
            else:
                move(src, out.at[here, :])

    def gd():
        for k in range(4):
            recv(("ch", k), hid.at[half(k, 1 - c), :])

        @pl.loop(0, 4)
        def _(m):
            there = (y + m) % 4
            g_down[pl.ds(al(there * 256, 256), 256), :] = lax.dot_general(
                hid[:, pl.ds(al(m * 256, 256), 256)], og[...].reshape(2048, 384), (((0,), (0,)), ((), ())),
                preferred_element_type=F32,
            ).astype(BF16)

        move(g_down, g_out)

    steps = (
        (stz, 1), (st_og, -1), (st_w, 0), (st_og, 0), (sty, 1), (fw, 1), (stz, 2), (ox, 3), (st_og, 1), (stz, 3),
        (st_w, 1), (sty, 0), (fw, 2), (fi, 1), (stz, 0), (b1, 0), (b1, 1), (fw, 3), (b2, 0), (fw, 0), (b1, 3),
        (sty, 2), (ox, 2), (g1, 1), (b2, 1), (b2, 3), (fi, 0), (g2, 1), (sty, 3), (fi, 2), (b1, 2), (g1, 0),
        (fi, 3), (b2, 2), (g2, 0), (g1, 2), (b3, 1), (g3, 1), (g1, 3), (g2, 2), (g3, 0), (g2, 3), (b3, 0),
        (e, 1), (b3, 3), (e, 0), (b3, 2), (a2x, 1), (g3, 2), (a2y, 1), (g3, 3), (a2x, 0), (e, 2), (afy, 1),
        (a3, 1), (a2x, 2), (a2y, 2), (a2y, 0), (e, 3), (a4, 1), (a3, 0), (xk, 1), (xk, 0), (a2x, 3), (a3, 2),
        (gp, 1), (a2y, 3), (xk, 2), (gp, 2), (a3, 3), (gp, 0), (x2, 0), (gf, 2), (afy, 0), (gf, 1), (afy, 2),
        (afy, 3), (gf, 3), (xk, 3), (x2, 2), (a4, 3), (x2, 1), (a4, 2), (a4, 0), (x2, 3), (gd,), (xt, 2),
        (xt, 0), (xt, 1), (gf, 0), (xt, 3),
    )
    for step in steps:
        step[0](*step[1:])

    for j in (1, 3, 2):
        for q, out in enumerate((g_gate, g_up)):
            recv(("gw", j, q), out.at[pl.ds(al(((x - j + 4) % 4) * 768, 256), 768), :])
    for copy in local[n_first:]:
        copy.wait()
    done = [id(copy) for copy in uses[:-N_SLOT]]
    for copy in sent:
        if id(copy) not in done:
            copy.wait_send()
    assert len(index) <= N_SEM, len(index)


def finish(*refs):
    ins, outs = [], []
    for k, (src, dst) in enumerate(zip(refs[:4], refs[4:8])):
        buf, n = refs[8 + k], src.shape[0] // 4
        for part in range(4):
            at = pl.ds(part * n, n)
            ins.append(pltpu.make_async_copy(src.at[at], buf.at[at], refs[12].at[len(ins)]))
            outs.append(pltpu.make_async_copy(buf.at[at], dst.at[at], refs[13].at[len(outs)]))
            ins[-1].start()
    for first, then in zip(ins, outs):
        first.wait()
        then.start()
    for then in outs:
        then.wait()


def shards(inputs, out_grad, w_gate, w_up, w_down):
    v = pltpu.VMEM
    any_ = pl.BlockSpec(memory_space=pl.ANY)
    outs = pl.pallas_call(
        kernel,
        name="swiglu_back",
        out_shape=(
            jax.ShapeDtypeStruct((256, 768), BF16),
            jax.ShapeDtypeStruct((3072, 128), BF16),
            jax.ShapeDtypeStruct((3072, 128), BF16),
            jax.ShapeDtypeStruct((1024, 384), BF16),
        ),
        in_specs=[any_] * 5,
        out_specs=(any_,) * 4,
        scratch_shapes=[
            v((2048, 768), BF16),
            v((768, 1024), BF16),
            v((4, 8, 4, 16, 384), BF16),
            v((1024, 384), BF16),
            v((N_SLOT, 512, 1024), F32),
            v((8, 256, 1024), F32),
            v((8, 256, 1024), BF16),
            v((4, 3, 256, 256), BF16),
            v((4, 3, 128, 128), BF16),
            v((4, 256, 256), F32),
            v((4, 128, 256), F32),
            v((4, 128, 128), F32),
            v((4, 3, 128, 512), BF16),
            v((4, 128, 512), BF16),
            v((2048, 1024), BF16),
            v((2048, 1024), BF16),
            v((4, 256, 768), BF16),
            v((4, 256, 768), BF16),
            v((max(1, len(DZ)), 256, 768), F32),
            v((max(1, len(DY)), 2, 4, 64, 768), F32),
            v((4, 2, 4, 64, 768), BF16),
            v((4, 3, 2, 64, 768), BF16),
            v((4, 768, 256), BF16),
            v((768, 1024), F32),
            v((256, 768), BF16),
            v((1024, 384), BF16),
            pltpu.SemaphoreType.DMA((N_SEM,)),
            pltpu.SemaphoreType.DMA((N_SEM,)),
            pltpu.SemaphoreType.DMA((20,)),
        ],
        compiler_params=pltpu.CompilerParams(collective_id=0, has_side_effects=True, vmem_limit_bytes=61 * 2**20),
        cost_estimate=pl.CostEstimate(flops=13 * 10**9, bytes_accessed=8 * 2**20, transcendentals=65536),
    )(inputs, out_grad.reshape(4, 4, 16, 3072), w_gate, w_up, w_down)
    return pl.pallas_call(
        finish,
        name="results",
        out_shape=tuple(jax.ShapeDtypeStruct(v.shape, v.dtype) for v in outs),
        in_specs=[any_] * 4,
        out_specs=(any_,) * 4,
        scratch_shapes=[v(o.shape, o.dtype) for o in outs] + [pltpu.SemaphoreType.DMA((16,))] * 2,
        cost_estimate=pl.CostEstimate(flops=0, bytes_accessed=5 * 2**20, transcendentals=0),
    )(*outs)


def solution(mesh):
    in_specs = (
        P("tok", "in"),
        P("tok", "in"),
        P("in", ("out", "tok")),
        P("in", ("out", "tok")),
        P("out", ("in", "tok")),
    )
    out_specs = (
        P("tok", ("in", "out")),
        P("in", ("out", "tok")),
        P("in", ("out", "tok")),
        P("out", ("in", "tok")),
    )
    return jax.shard_map(shards, mesh=mesh, in_specs=in_specs, out_specs=out_specs, check_vma=False)
```
